256 devices in a mesh: gr: 16 (over z, core), gc: 16 (over x, y).
Axes of the slice: x: 4, y: 4, z: 8, core: 2. Of those that a mesh axis runs over, the one named last changes fastest.
Arguments:
- out_grad: bfloat16 [131072, 512], P(('gr', 'gc')), may hold values from -6 to 6
- preactivation_state: bfloat16 [131072, 512], P(('gr', 'gc')), may hold values from -6 to 6
- features: bfloat16 [131072, 512], P(('gc', 'gr')), may hold values from -24 to 24
- weight: bfloat16 [512, 512], replicated, may hold values from -0.25 to 0.25
- block_values: bfloat16 [16, 16, 152, 128, 128], P('gr', 'gc'), may hold values from -0.1875 to 0.1875
- block_rows: int32 [16, 16, 152], P('gr', 'gc'), may hold values from 0 to 63, as said below
- block_cols: int32 [16, 16, 152], P('gr', 'gc'), may hold values from 0 to 63, as said below
- block_counts: int32 [16, 16], P('gr', 'gc'), may hold values from 1 to 152, as said below
Outputs:
- input_grad: bfloat16 [131072, 512], P(('gc', 'gr'))
- weight_grad: float32 [512, 512], replicated
The draws below stay inside these ranges and needn't reach their ends.
Inputs may be any that keep to these rules, and one draw needn't show every extreme that they name: `block_rows`: block row within a tile; some entry equals 63. `block_cols`: block column within a tile; some entry equals 63. `block_counts`: slots from this count on are unused; some tile uses all 152 slots.
All inputs are finite; a program needn't handle non-finite values.
Results may differ from the reference program's by a relative error of at most 0.014.
Values may be sent and summed in bfloat16 or wider, within the bound.
A program may use at most 128 MiB of HBM per device.

```python
import jax
import jax.numpy as jnp
from jax import lax

D = 512
BLOCK = 128
ROWS_DEV = 512
BMAX = 152
NODES = 131072
ROW_BLOCKS = 64
COL_BLOCKS = 64
N_GR = 16
N_GC = 16


def draw_block_counts(key, part):
    first, second, third = jax.random.split(jax.random.fold_in(key, 11), 3)
    left = jax.random.randint(first, (N_GR, N_GC), 1, BMAX + 1)
    right = jax.random.randint(second, (N_GR, N_GC), 1, BMAX + 1)
    counts = (left * right + BMAX - 1) // BMAX
    peak = jax.random.randint(third, (), 0, N_GR * N_GC)
    places = jnp.arange(N_GR * N_GC).reshape(N_GR, N_GC)
    return jnp.where(places == peak, BMAX, counts).astype(jnp.int32)


def draw_block_rows(key, part):
    picks = jax.random.randint(jax.random.fold_in(key, 12), (N_GR, N_GC, BMAX), 0, ROW_BLOCKS)
    return picks.at[0, 0, 0].set(ROW_BLOCKS - 1).astype(jnp.int32)


def draw_block_cols(key, part):
    picks = jax.random.randint(jax.random.fold_in(key, 13), (N_GR, N_GC, BMAX), 0, COL_BLOCKS)
    return picks.at[0, 0, 0].set(COL_BLOCKS - 1).astype(jnp.int32)


def strengthened(array, own_key, source, target, parts, factor):
    def block_of(axis_at):
        return (jnp.arange(array.shape[axis_at]) // (array.shape[axis_at] // parts)).reshape((-1,) + (1,) * (array.ndim - 1 - axis_at))

    near = jax.random.permutation(own_key, parts)[block_of(target)]
    far = (block_of(target) + parts // 2) % parts
    return jnp.where((block_of(source) == near) | (block_of(source) == far), factor * array, array)


def block_scale(key, extent, cuts, smallest, largest):
    level, own = 1.0, jax.random.fold_in(key, 6)
    for position, shards_of in cuts:
        steps = jnp.exp(jax.random.uniform(jax.random.fold_in(own, position), (shards_of,), jnp.float32, smallest / len(cuts), largest / len(cuts)))
        level = level * jnp.repeat(steps, extent[position] // shards_of).reshape([-1 if axis == position else 1 for axis in range(len(extent))])
    return level


def scatter_about(key, shape, deviation, reach, pieces=(), held_as=jnp.bfloat16):
    result = deviation * jax.random.normal(key, shape, jnp.float32)
    if pieces:
        result = result * block_scale(key, shape, pieces, -0.22, 0.18)
    return jnp.clip(result, -reach, reach).astype(held_as)


def gaussian_with(key, dims, scale, bound, cuts, heavy, kind=jnp.bfloat16):
    drawn = scale * jax.random.normal(key, dims, jnp.float32)
    if cuts:
        drawn = drawn * block_scale(key, dims, cuts, -0.22, 0.18)
    return jnp.clip(strengthened(drawn, jax.random.fold_in(key, 3), *heavy), -bound, bound).astype(kind)


def setup_inputs(seed: int = 0) -> dict:
    arg_keys = jax.random.split(jax.random.key(seed), 9)
    out_grad = scatter_about(arg_keys[0], (NODES, D), 1.0, 6.0, ((0, 256),))
    preactivation_state = scatter_about(arg_keys[1], (NODES, D), 1.0, 6.0, ((0, 256),))
    features = gaussian_with(arg_keys[2], (NODES, D), 1.0, 24.0, ((0, 256),), (0, 1, 256, 6.0))
    weight = scatter_about(arg_keys[3], (D, D), D ** -0.5, 0.25)
    block_values = scatter_about(arg_keys[4], (N_GR, N_GC, BMAX, BLOCK, BLOCK), (BLOCK * 8) ** -0.5, 0.1875, ((0, 16), (1, 16)))
    block_rows = draw_block_rows(jax.random.fold_in(arg_keys[8], 71), 0)
    block_cols = draw_block_cols(jax.random.fold_in(arg_keys[8], 71), 0)
    block_counts = draw_block_counts(jax.random.fold_in(arg_keys[8], 71), 0)
    return {"out_grad": out_grad, "preactivation_state": preactivation_state, "features": features, "weight": weight, "block_values": block_values, "block_rows": block_rows, "block_cols": block_cols, "block_counts": block_counts}


def tile_partial(masked, block_values, block_rows, block_cols, block_counts, tile_row, tile_col):
    tile_height = ROWS_DEV * N_GC
    offset = (tile_row * tile_height).astype(jnp.int32)
    rows_now = lax.dynamic_slice_in_dim(masked, offset, tile_height, 0).reshape(ROW_BLOCKS, BLOCK, D)
    current_values = block_values[tile_row, tile_col]
    selected_entries = rows_now[block_rows[tile_row, tile_col]]
    contribution = jnp.einsum('yql,yqa->yla', current_values.astype(jnp.float32), selected_entries.astype(jnp.float32))
    active = jnp.arange(BMAX) < block_counts[tile_row, tile_col]
    contribution = jnp.where(active[:, None, None], contribution, jnp.zeros_like(contribution))
    value_partial_sum = jnp.zeros((COL_BLOCKS, BLOCK, D), jnp.float32).at[block_cols[tile_row, tile_col]].add(contribution)
    return value_partial_sum.reshape(COL_BLOCKS * BLOCK, D).astype(jnp.bfloat16)


def reference(out_grad, preactivation_state, features, weight, block_values, block_rows, block_cols, block_counts):
    masked = jnp.where(preactivation_state > 0, out_grad, jnp.zeros_like(out_grad)).astype(jnp.bfloat16)

    def column_sum(tile_col):
        def add_tile(tile_row, total):
            return total + tile_partial(masked, block_values, block_rows, block_cols, block_counts, tile_row, tile_col).astype(jnp.float32)
        return lax.fori_loop(0, N_GR, add_tile, jnp.zeros((ROWS_DEV * N_GR, D), jnp.float32))

    totals = lax.map(column_sum, jnp.arange(N_GC, dtype=jnp.int32))
    spread = totals.reshape(NODES, D).astype(jnp.bfloat16)
    input_grad = jnp.dot(spread, weight.T, preferred_element_type=jnp.float32).astype(jnp.bfloat16)
    weight_grad = jnp.dot(features.T, spread, preferred_element_type=jnp.float32) * (NODES ** -0.5)
    return input_grad, weight_grad
```

```python
import functools

import jax
import jax.numpy as jnp
from jax import lax
from jax.experimental import pallas as pl
from jax.experimental.pallas import tpu as pltpu
from jax.sharding import PartitionSpec as P

MESH = pl.DeviceIdType.MESH
B = 128
SLOTS = 152
CHUNKS = 4
UNROLL = 19
BF = jnp.bfloat16
F32 = jnp.float32


def kernel(
    packed, last, og_h, pre_h, feat_h, w_h, vals_h,
    ig_o, wg_o,
    g0, g1, g2, g3, og, pre, feat, w, vals, prods, part, sib, zs, zr, spread, term, tsend, trecv,
    psend, precv, zx, wg,
    local_sem, g_send, g_recv, e_send, e_recv, z_send, z_recv, t_send, t_recv, p_send, p_recv,
    x_send, x_recv, q_send, q_recv, c_send, c_recv,
):
    gathered = (g0, g1, g2, g3)
    gr, gc = lax.axis_index("gr"), lax.axis_index("gc")
    z, core = gr // 2, gr % 2
    x, y = gc // 4, gc % 4
    sibling = {"gr": z * 2 + (1 - core), "gc": gc}

    def z_peer(d):
        return {"gr": ((z + d) % 8) * 2 + core, "gc": gc}

    def plane_peer(d):
        return {"gr": gr, "gc": (gc + d) % 16}

    def x_peer(d):
        return {"gr": gr, "gc": ((x + d + 4) % 4) * 4 + y}

    def y_peer(d):
        return {"gr": gr, "gc": x * 4 + (y + d + 4) % 4}

    loads = [
        pltpu.make_async_copy(og_h, og, local_sem.at[0]),
        pltpu.make_async_copy(pre_h, pre, local_sem.at[1]),
        pltpu.make_async_copy(vals_h, vals, local_sem.at[2]),
        pltpu.make_async_copy(feat_h, feat, local_sem.at[3]),
        pltpu.make_async_copy(w_h, w, local_sem.at[4]),
    ]
    for load in loads:
        load.start()

    barrier = pltpu.get_barrier_semaphore()
    pl.semaphore_signal(barrier, inc=1, device_id=sibling, device_id_type=MESH)

    def greet_z(d, _):
        pl.semaphore_signal(barrier, inc=1, device_id=z_peer(d), device_id_type=MESH)
        return 0

    def greet_plane(d, _):
        pl.semaphore_signal(barrier, inc=1, device_id=plane_peer(d), device_id_type=MESH)
        return 0

    lax.fori_loop(1, 8, greet_z, 0)
    lax.fori_loop(1, 16, greet_plane, 0)

    ring = (x, y)
    cross = (y, x)
    near = (x_peer, y_peer)
    far = (y_peer, x_peer)

    def unit(h, p, q):
        return h * 32 + p * 8 + q * 2

    loads[0].wait()
    loads[1].wait()
    for k in range(CHUNKS):
        for b in range(4):
            rows, cols = pl.ds(b * B, B), pl.ds(k * B, B)
            block = og[rows, cols]
            block = jnp.where(pre[rows, cols].astype(F32) > 0, block.astype(F32), 0.0)
            h = b // 2
            gathered[k][unit(h, cross[h], ring[h]) + b % 2] = block.T.astype(BF)
    prods[SLOTS] = jnp.zeros((B, B), BF)
    pl.semaphore_wait(barrier, 23)

    sent = []
    pending = {}

    def send(key, src, dst, send_sem, recv_sem, device):
        copy = pltpu.make_async_remote_copy(
            src_ref=src, dst_ref=dst, send_sem=send_sem, recv_sem=recv_sem, device_id=device, device_id_type=MESH
        )
        copy.start()
        sent.append(copy)
        pending[key] = copy

    def arrived(key):
        pending.pop(key).wait_recv()

    def gather_copy(stage, k, h, d, at, size, device):
        n = ((k * 5 + stage) * 2 + h) * 2 + (d + 1) // 2
        where = gathered[k].at[pl.ds(at, size)]
        send(("g", stage, k, h, d), where, where, g_send.at[n], g_recv.at[n], device)

    def first_ring(k):
        for h in range(2):
            for d in (1, -1):
                gather_copy(0, k, h, d, unit(h, cross[h], ring[h]), 2, near[h](d))

    def first_forward(k):
        for h in range(2):
            for d in (1, -1):
                arrived(("g", 0, k, h, d))
                came = (ring[h] - d + 4) % 4
                gather_copy(1, k, h, d, unit(h, cross[h], came) + (0 if d == 1 else 1), 1, near[h](d))

    def second_ring(k):
        for h in range(2):
            for d in (1, -1):
                arrived(("g", 1, k, h, d))
            for part_no in range(2):
                for d in (1, -1):
                    which = part_no if d == 1 else 1 - part_no
                    gather_copy(2 + part_no, k, h, d, unit(h, cross[h], 0) + 4 * which, 4, far[h](d))

    def second_forward(k):
        for h in range(2):
            for d in (1, -1):
                arrived(("g", 2, k, h, d))
                came = (cross[h] - d + 4) % 4
                gather_copy(4, k, h, d, unit(h, came, 0) + (0 if d == 1 else 4), 4, far[h](d))

    def gather_end(k):
        for stage in (3, 4):
            for h in range(2):
                for d in (1, -1):
                    arrived(("g", stage, k, h, d))

    order = (4, 3, 5, 2, 6, 1, 7, 0)

    def multiply(k):
        source = gathered[k]

        def some(t, total):
            for u in range(UNROLL):
                s = t * UNROLL + u
                word = packed[s]
                term_now = jnp.dot(source[(word >> 8) & 255], vals[word & 255], preferred_element_type=F32)
                total = jnp.where((word >> 16) != 0, term_now, total + term_now)
                prods[s] = total.astype(BF)
            return total

        lax.fori_loop(0, SLOTS // UNROLL, some, jnp.zeros((B, B), F32))
        for d in order:
            zp = (z + d) % 8

            def place(j, _):
                part[k, zp * 8 + j] = prods[last[zp * 8 + j]]
                return 0

            lax.fori_loop(0, 8, place, 0, unroll=True)
            n = k * 8 + d
            send(
                ("e", k, d), part.at[k, pl.ds(zp * 8 + (1 - core) * 4, 4)], sib.at[k, pl.ds(zp * 4, 4)],
                e_send.at[n], e_recv.at[n], sibling,
            )

    def own(k, zp, b):
        return part[k, zp * 8 + core * 4 + b].astype(F32) + sib[k, zp * 4 + b].astype(F32)

    def z_copy(k, side, t, low, size):
        n = (k * 2 + side) * 4 + t - 1
        send(
            ("z", k, side, t), zs.at[n, pl.ds(low, size)], zr.at[n, pl.ds(low, size)],
            z_send.at[n], z_recv.at[n], z_peer(7 if side == 0 else 1),
        )

    def z_step(k, t):
        if t == 4:
            arrived(("e", k, 4))
            zp = (z + 4) % 8
            for side in range(2):
                n = (k * 2 + side) * 4 + 3
                for b in (2 * side, 2 * side + 1):
                    zs[n, b] = own(k, zp, b).astype(BF)
                z_copy(k, side, 4, 2 * side, 2)
            return
        for side in range(2):
            d = 8 - t if side == 0 else t
            zp = (z + d) % 8
            n = (k * 2 + side) * 4 + t - 1
            arrived(("e", k, d))
            arrived(("z", k, side, t + 1))
            for b in range(4):
                value = own(k, zp, b)
                if t < 3 or b // 2 == side:
                    value = value + zr[n + 1, b].astype(F32)
                zs[n, b] = value.astype(BF)
            z_copy(k, side, t, 0, 4)

    def z_end(k):
        arrived(("e", k, 0))
        arrived(("z", k, 0, 1))
        arrived(("z", k, 1, 1))
        for b in range(4):
            total = own(k, z, b) + zr[k * 8, b].astype(F32) + zr[k * 8 + 4, b].astype(F32)
            spread[k * 4 + b] = total.astype(BF)

    def weight_term(k):
        total = jnp.dot(spread[k * 4], feat[pl.ds(0, B), :], preferred_element_type=F32)
        for b in range(1, 4):
            total = total + jnp.dot(spread[k * 4 + b], feat[pl.ds(b * B, B), :], preferred_element_type=F32)
        term[k] = total
        tsend[k] = term[k, pl.ds((1 - core) * 64, 64), :].astype(BF)
        send(("t", k), tsend.at[k], trecv.at[k], t_send.at[k], t_recv.at[k], sibling)

    def plane_scatter(k):
        arrived(("t", k))
        for a in range(4):
            for b in range(4):
                lanes = pl.ds(b * B, B)
                mine = term[k, pl.ds(core * 64 + a * 16, 16), lanes]
                psend[k, a * 4 + b] = (mine + trecv[k, pl.ds(a * 16, 16), lanes].astype(F32)).astype(BF)
        for o in range(1, 16):
            n = k * 15 + o - 1
            to = plane_peer(o)
            send(("p", k, o), psend.at[k, to["gc"]], precv.at[k, o - 1], p_send.at[n], p_recv.at[n], to)

    def z_exchange(k):
        total = psend[k, gc].astype(F32)
        for o in range(1, 16):
            arrived(("p", k, o))
            total = total + precv[k, o - 1].astype(F32)
        zx[k, z] = total.astype(BF)
        for o in range(1, 8):
            n = k * 7 + o - 1
            send(("x", k, o), zx.at[k, z], zx.at[k, z], x_send.at[n], x_recv.at[n], z_peer(o))

    def plane_gather(k):
        for o in range(1, 8):
            arrived(("x", k, o))
        total = zx[k, 0].astype(F32)
        for a in range(1, 8):
            total = total + zx[k, a].astype(F32)
        wg[k, core, gc] = total.astype(BF)
        for o in range(1, 16):
            n = k * 15 + o - 1
            send(("q", k, o), wg.at[k, core, gc], wg.at[k, core, gc], q_send.at[n], q_recv.at[n], plane_peer(o))

    def core_gather(k):
        for o in range(1, 16):
            arrived(("q", k, o))
        send(("c", k), wg.at[k, core], wg.at[k, core], c_send.at[k], c_recv.at[k], sibling)

    def weight_out(k):
        arrived(("c", k))
        for c in range(2):
            for a in range(4):
                for b in range(4):
                    wg_o[pl.ds(k * B + c * 64 + a * 16, 16), pl.ds(b * B, B)] = wg[k, c, a * 4 + b]

    def input_rows(b):
        total = jnp.zeros((B, 512), F32)
        for k in range(CHUNKS):
            total = total + lax.dot_general(
                spread[k * 4 + b].T, w[:, pl.ds(k * B, B)], (((1,), (1,)), ((), ())), preferred_element_type=F32
            )
        ig_o[pl.ds(b * B, B), :] = total.astype(BF)

    first_ring(0)
    first_ring(1)
    first_forward(0)
    second_ring(0)
    first_forward(1)
    first_ring(2)
    second_forward(0)
    second_ring(1)
    first_forward(2)
    first_ring(3)
    for load in loads[2:]:
        load.wait()
    gather_end(0)

    multiply(0)
    second_forward(1)
    second_ring(2)
    first_forward(3)
    z_step(0, 4)
    z_step(0, 3)
    z_step(0, 2)
    gather_end(1)

    multiply(1)
    z_step(0, 1)
    second_forward(2)
    second_ring(3)
    z_end(0)
    weight_term(0)
    z_step(1, 4)
    plane_scatter(0)
    z_step(1, 3)
    z_exchange(0)
    z_step(1, 2)
    plane_gather(0)
    gather_end(2)

    multiply(2)
    z_step(1, 1)
    second_forward(3)
    core_gather(0)
    z_end(1)
    weight_term(1)
    z_step(2, 4)
    plane_scatter(1)
    z_step(2, 3)
    z_exchange(1)
    z_step(2, 2)
    plane_gather(1)
    gather_end(3)

    multiply(3)
    z_step(2, 1)
    core_gather(1)
    z_end(2)
    weight_term(2)
    z_step(3, 4)
    plane_scatter(2)
    z_step(3, 3)
    z_exchange(2)
    z_step(3, 2)
    plane_gather(2)
    z_step(3, 1)
    weight_out(0)
    weight_out(1)
    core_gather(2)
    z_end(3)
    weight_term(3)
    plane_scatter(3)
    input_rows(0)
    input_rows(1)
    z_exchange(3)
    input_rows(2)
    plane_gather(3)
    input_rows(3)
    weight_out(2)
    core_gather(3)
    for copy in sent:
        copy.wait_send()
    weight_out(3)


def local(out_grad, state, features, weight, block_values, block_rows, block_cols, block_counts):
    values, rows, cols, count = block_values[0, 0], block_rows[0, 0], block_cols[0, 0], block_counts[0, 0]
    slot = jnp.arange(SLOTS, dtype=jnp.int32)
    key = jnp.where(slot < count, cols, 64)
    before = (key[None, :] < key[:, None]) | ((key[None, :] == key[:, None]) & (slot[None, :] < slot[:, None]))
    rank = jnp.sum(before.astype(jnp.int32), axis=1)
    first = jnp.sum(((key[None, :] == key[:, None]) & (slot[None, :] < slot[:, None])).astype(jnp.int32), axis=1) == 0
    device, b = rows // 4, rows % 4
    a0, a1 = device // 4, device % 4
    place = jnp.where(b < 2, a1 * 8 + a0 * 2 + b, 32 + a0 * 8 + a1 * 2 + b - 2)
    word = slot | (place << 8) | (first.astype(jnp.int32) << 16)
    packed = jnp.sum(jnp.where(rank[None, :] == slot[:, None], word[None, :], 0), axis=1)
    column = jnp.arange(64, dtype=jnp.int32)
    upto = jnp.sum((key[None, :] <= column[:, None]).astype(jnp.int32), axis=1)
    here = jnp.sum((key[None, :] == column[:, None]).astype(jnp.int32), axis=1)
    last = jnp.where(here > 0, upto - 1, SLOTS)

    anywhere = pl.BlockSpec(memory_space=pl.ANY)
    dma = pltpu.SemaphoreType.DMA
    grid = (512, 512)
    ig, wg = pl.pallas_call(
        kernel,
        out_shape=(jax.ShapeDtypeStruct(grid, BF), jax.ShapeDtypeStruct(grid, BF)),
        in_specs=[pl.BlockSpec(memory_space=pltpu.SMEM)] * 2 + [anywhere] * 5,
        out_specs=(pl.BlockSpec(memory_space=pltpu.VMEM), pl.BlockSpec(memory_space=pltpu.VMEM)),
        scratch_shapes=[pltpu.VMEM((64, B, B), BF)] * 4
        + [pltpu.VMEM(grid, BF)] * 4
        + [
            pltpu.VMEM((SLOTS, B, B), BF),
            pltpu.VMEM((SLOTS + 1, B, B), BF),
            pltpu.VMEM((CHUNKS, 64, B, B), BF),
            pltpu.VMEM((CHUNKS, 32, B, B), BF),
            pltpu.VMEM((CHUNKS * 8, 4, B, B), BF),
            pltpu.VMEM((CHUNKS * 8, 4, B, B), BF),
            pltpu.VMEM((CHUNKS * 4, B, B), BF),
            pltpu.VMEM((CHUNKS, B, 512), F32),
            pltpu.VMEM((CHUNKS, 64, 512), BF),
            pltpu.VMEM((CHUNKS, 64, 512), BF),
            pltpu.VMEM((CHUNKS, 16, 16, B), BF),
            pltpu.VMEM((CHUNKS, 15, 16, B), BF),
            pltpu.VMEM((CHUNKS, 8, 16, B), BF),
            pltpu.VMEM((CHUNKS, 2, 16, 16, B), BF),
            dma((5,)),
            dma((CHUNKS * 20,)),
            dma((CHUNKS * 20,)),
            dma((CHUNKS * 8,)),
            dma((CHUNKS * 8,)),
            dma((CHUNKS * 8,)),
            dma((CHUNKS * 8,)),
            dma((CHUNKS,)),
            dma((CHUNKS,)),
            dma((CHUNKS * 15,)),
            dma((CHUNKS * 15,)),
            dma((CHUNKS * 7,)),
            dma((CHUNKS * 7,)),
            dma((CHUNKS * 15,)),
            dma((CHUNKS * 15,)),
            dma((CHUNKS,)),
            dma((CHUNKS,)),
        ],
        compiler_params=pltpu.CompilerParams(
            collective_id=0, has_side_effects=True, vmem_limit_bytes=56 * 1024 * 1024
        ),
        name="graph_backward",
    )(packed, last, out_grad, state, features, weight, values)
    nodes = 512 * lax.axis_size("gr") * lax.axis_size("gc")
    return ig, wg.T.astype(F32) * nodes ** (-0.5)


def solution(mesh):
    in_specs = (
        P(("gr", "gc"), None),
        P(("gr", "gc"), None),
        P(("gc", "gr"), None),
        P(),
        P("gr", "gc", None, None, None),
        P("gr", "gc", None),
        P("gr", "gc", None),
        P("gr", "gc"),
    )
    out_specs = (P(("gc", "gr"), None), P())
    return jax.shard_map(local, mesh=mesh, in_specs=in_specs, out_specs=out_specs, check_vma=False)
```

```python
import functools

import jax
import jax.numpy as jnp
from jax import lax
from jax.experimental import pallas as pl
from jax.experimental.pallas import tpu as pltpu
from jax.sharding import PartitionSpec as P

MESH = pl.DeviceIdType.MESH
B = 128
SLOTS = 152
CUTS = ((0, 64), (64, 64), (128, 128), (256, 128), (384, 64), (448, 64))
CHUNKS = len(CUTS)
UNITS = 4
UNROLL = 19
BF = jnp.bfloat16
F32 = jnp.float32


GROUPS = ((4,), (3, 5), (2, 6), (1, 7), (0,))


def plan():
    tasks = {}

    def task(name, args, after=(), needs=(), sends=(), cost=0.1, rank=0.0):
        tasks[name, args] = (tuple(after), tuple(needs), tuple(sends), cost, rank)

    chip, core = 2.4, 0.9
    task("loads", (), cost=0.1, rank=0)
    for k, (at, size) in enumerate(CUTS):
        unit = size / 2
        task("ring1", (k,), [("ring1", (k - 1,))] if k else [], (), [(("r1", k), "xy", unit, chip)], rank=-9)
        task("pass1", (k,), [], [("r1", k)], [(("f1", k), "xy", unit / 2, chip)], rank=-8)
        before = max(0, k - 1 - (size == 64))
        gate = [("pass2", (before,))] if k > 1 else []
        task(
            "ring2", (k,), gate + ([("ring2", (k - 1,))] if k else []), [("f1", k)],
            [(("a", k), "xy", unit * 2, chip), (("b", k), "xy", unit * 2, chip)], rank=-7,
        )
        task("pass2", (k,), [], [("a", k)], [(("f2", k), "xy", unit * 2, chip)], rank=-8)
        load = 0.5 + size / 128
        follow = [("place", (k - 1, GROUPS[-1]))] if k else [("loads", ())]
        task("mult", (k, 0), follow, [("b", k), ("f2", k)], cost=load, rank=k)
        task("mult", (k, 1), [("mult", (k, 0))], cost=load, rank=k)
        for i, group in enumerate(GROUPS):
            task(
                "place", (k, group), [("place", (k, GROUPS[i - 1])) if i else ("mult", (k, 1))], (),
                [(("e", k, d), "core", size, core) for d in group], 0.08 * len(group), k - 0.5,
            )
        for chain in range(2):
            for t in range(4 - chain, 0, -1):
                needs = [("e", k, d) for d in {t, 8 - t}]
                if t < 4 - chain:
                    needs.append(("z", k, chain, t + 1))
                task("z", (k, chain, t), (), needs, [(("z", k, chain, t), "z", size / 2, chip)], 0.2, -6 + k / 10)
        task("zend", (k,), (), [("e", k, 0), ("z", k, 0, 1), ("z", k, 1, 1)], cost=0.25, rank=-5 + k / 10)
    for u in range(UNITS):
        ends = [("zend", (k,)) for k, (at, _) in enumerate(CUTS) if at // B == u]
        task("term", (u,), ends, (), [(("t", u), "core", 64, core)], 0.7, u - 1)
        task("scatter", (u,), (), [("t", u)], [(("p", u), "xy", 32, 4.5)], 0.5, u - 1)
        task("zsum", (u,), (), [("p", u)], [(("x", u), "z", 32, 4.5)], 0.4, u - 1)
        task("gather", (u,), (), [("x", u)], [(("q", u), "xy", 32, 4.5)], 0.5, u - 1)
        task("core", (u,), (), [("q", u)], [(("c", u), "core", 64, core)], 0.2, u - 1)
        task("out", (u,), (), [("c", u)], cost=0.4, rank=u + 1)
    for b in range(4):
        task("rows", (b,), [("zend", (CHUNKS - 1,)), ("scatter", (UNITS - 1,))], cost=0.6, rank=20)
    for i, stage in enumerate(("zend", "zsum", "gather")):
        stage_args = (CHUNKS - 2,) if stage == "zend" else (UNITS - 1,)
        task("drain", (i,), [(stage, stage_args)], cost=1.0, rank=30)

    now, free, come, done, order = 0.0, {"xy": 0.0, "z": 0.0, "core": 0.0}, {}, set(), []
    rate = {"xy": 48.0, "z": 48.0, "core": 600.0}
    while tasks:
        best = None
        for key, (after, needs, _, cost, rank) in tasks.items():
            if all(a in done for a in after) and all(n in come for n in needs):
                ready = max([now] + [come[n] for n in needs])
                score = (ready, rank)
                if best is None or score < best[0]:
                    best = (score, key)
        (now, _), key = best
        _, _, sends, cost, _ = tasks.pop(key)
        now += cost
        for message, link, kib, latency in sends:
            free[link] = max(free[link], now) + kib / rate[link]
            come[message] = free[link] + latency
        done.add(key)
        order.append(key)
    return order


def kernel(
    packed, last, og_h, pre_h, feat_h, w_h, vals_h,
    ig_o, wg_o,
    g0, g1, g2, g3, g4, g5, og, pre, feat, w, vals, prods, carry, part, sib, zs, zr, spread, term, tsend, trecv,
    psend, precv, zx, wg,
    local_sem, g_send, g_recv, e_send, e_recv, z_send, z_recv, t_send, t_recv, p_send, p_recv,
    x_send, x_recv, q_send, q_recv, c_send, c_recv,
):
    gathered = (g0, g1, g2, g3, g4, g5)
    gr, gc = lax.axis_index("gr"), lax.axis_index("gc")
    z, core = gr // 2, gr % 2
    x, y = gc // 4, gc % 4
    sibling = {"gr": z * 2 + (1 - core), "gc": gc}

    def z_peer(d):
        return {"gr": ((z + d) % 8) * 2 + core, "gc": gc}

    def plane_peer(d):
        return {"gr": gr, "gc": (gc + d) % 16}

    def x_peer(d):
        return {"gr": gr, "gc": ((x + d + 4) % 4) * 4 + y}

    def y_peer(d):
        return {"gr": gr, "gc": x * 4 + (y + d + 4) % 4}

    loads = [
        pltpu.make_async_copy(og_h, og, local_sem.at[0]),
        pltpu.make_async_copy(pre_h, pre, local_sem.at[1]),
        pltpu.make_async_copy(vals_h, vals, local_sem.at[2]),
        pltpu.make_async_copy(feat_h, feat, local_sem.at[3]),
        pltpu.make_async_copy(w_h, w, local_sem.at[4]),
    ]
    for load in loads:
        load.start()

    barrier = pltpu.get_barrier_semaphore()
    pl.semaphore_signal(barrier, inc=1, device_id=sibling, device_id_type=MESH)

    def greet_z(d, _):
        pl.semaphore_signal(barrier, inc=1, device_id=z_peer(d), device_id_type=MESH)
        return 0

    def greet_plane(d, _):
        pl.semaphore_signal(barrier, inc=1, device_id=plane_peer(d), device_id_type=MESH)
        return 0

    lax.fori_loop(1, 8, greet_z, 0)
    lax.fori_loop(1, 16, greet_plane, 0)

    ring = (x, y)
    cross = (y, x)
    near = (x_peer, y_peer)
    far = (y_peer, x_peer)

    def unit(h, p, q):
        return h * 32 + p * 8 + q * 2

    loads[0].wait()
    loads[1].wait()
    for k in range(UNITS):
        for b in range(4):
            rows, cols = pl.ds(b * B, B), pl.ds(k * B, B)
            block = og[rows, cols]
            block = jnp.where(pre[rows, cols].astype(F32) > 0, block.astype(F32), 0.0).T.astype(BF)
            h = b // 2
            for n, (at, size) in enumerate(CUTS):
                if at // B == k:
                    gathered[n][unit(h, cross[h], ring[h]) + b % 2] = block[at % B : at % B + size]
    prods[SLOTS] = jnp.zeros((B, B), BF)
    pl.semaphore_wait(barrier, 23)

    sent = []
    pending = {}

    def send(key, src, dst, send_sem, recv_sem, device):
        copy = pltpu.make_async_remote_copy(
            src_ref=src, dst_ref=dst, send_sem=send_sem, recv_sem=recv_sem, device_id=device, device_id_type=MESH
        )
        copy.start()
        sent.append(copy)
        pending[key] = copy

    def arrived(key):
        pending.pop(key).wait_recv()

    def gather_copy(stage, k, h, d, at, size, device):
        n = ((k * 5 + stage) * 2 + h) * 2 + (d + 1) // 2
        where = gathered[k].at[pl.ds(at, size)]
        send(("g", stage, k, h, d), where, where, g_send.at[n], g_recv.at[n], device)

    def first_ring(k):
        for h in range(2):
            for d in (1, -1):
                gather_copy(0, k, h, d, unit(h, cross[h], ring[h]), 2, near[h](d))

    def first_forward(k):
        for h in range(2):
            for d in (1, -1):
                arrived(("g", 0, k, h, d))
                came = (ring[h] - d + 4) % 4
                gather_copy(1, k, h, d, unit(h, cross[h], came) + (0 if d == 1 else 1), 1, near[h](d))

    def second_ring(k):
        for h in range(2):
            for d in (1, -1):
                arrived(("g", 1, k, h, d))
        for part_no in range(2):
            for h in range(2):
                for d in (1, -1):
                    which = part_no if d == 1 else 1 - part_no
                    gather_copy(2 + part_no, k, h, d, unit(h, cross[h], 0) + 4 * which, 4, far[h](d))

    def second_forward(k):
        for h in range(2):
            for d in (1, -1):
                arrived(("g", 2, k, h, d))
                came = (cross[h] - d + 4) % 4
                gather_copy(4, k, h, d, unit(h, came, 0) + (0 if d == 1 else 4), 4, far[h](d))

    def multiply(k, half):
        at, size = CUTS[k]
        source = gathered[k]
        if half == 0:
            for stage in (3, 4):
                for h in range(2):
                    for d in (1, -1):
                        arrived(("g", stage, k, h, d))

        def some(t, total):
            for u in range(UNROLL):
                s = (half * 4 + t) * UNROLL + u
                word = packed[s]
                term_now = jnp.dot(source[(word >> 8) & 255], vals[word & 255], preferred_element_type=F32)
                total = jnp.where((word >> 16) != 0, term_now, total + term_now)
                prods[s, pl.ds(0, size)] = total.astype(BF)
            return total

        begin = jnp.zeros((size, B), F32) if half == 0 else carry[pl.ds(0, size), :]
        total = lax.fori_loop(0, SLOTS // UNROLL // 2, some, begin)
        if half == 0:
            carry[pl.ds(0, size), :] = total

    def place(k, group):
        at, size = CUTS[k]
        for d in group:
            zp = (z + d) % 8

            def one(j, _):
                part[zp * 8 + j, pl.ds(at, size)] = prods[last[zp * 8 + j], pl.ds(0, size)]
                return 0

            lax.fori_loop(0, 8, one, 0, unroll=True)
            n = k * 8 + d
            send(
                ("e", k, d),
                part.at[pl.ds(zp * 8 + (1 - core) * 4, 4), pl.ds(at, size)],
                sib.at[pl.ds(zp * 4, 4), pl.ds(at, size)],
                e_send.at[n], e_recv.at[n], sibling,
            )

    exchanged = set()

    def own(k, d, b):
        if (k, d) not in exchanged:
            exchanged.add((k, d))
            arrived(("e", k, d))
        zp = (z + d) % 8
        cut = pl.ds(*CUTS[k])
        return part[zp * 8 + core * 4 + b, cut].astype(F32) + sib[zp * 4 + b, cut].astype(F32)

    def z_step(k, chain, t):
        cut = pl.ds(*CUTS[k])
        for side in range(2):
            h = side if chain == 0 else 1 - side
            d = 8 - t if side == 0 else t
            n = side * 4 + t - 1
            fresh = t == 4 - chain
            if not fresh:
                arrived(("z", k, chain, side, t + 1))
            for b in (2 * h, 2 * h + 1):
                value = own(k, d, b)
                if not fresh:
                    value = value + zr[n + 1, b, cut].astype(F32)
                zs[n, b, cut] = value.astype(BF)
            m = (k * 2 + side) * 7 + (t + 2 if chain == 0 else t - 1)
            blocks = pl.ds(2 * h, 2)
            send(
                ("z", k, chain, side, t), zs.at[n, blocks, cut], zr.at[n, blocks, cut],
                z_send.at[m], z_recv.at[m], z_peer(7 if side == 0 else 1),
            )

    def z_end(k):
        cut = pl.ds(*CUTS[k])
        for chain in range(2):
            for side in range(2):
                arrived(("z", k, chain, side, 1))
        for b in range(4):
            total = own(k, 0, b) + zr[0, b, cut].astype(F32) + zr[4, b, cut].astype(F32)
            spread[b, cut] = total.astype(BF)

    def weight_term(k):
        total = jnp.dot(spread[0, pl.ds(k * B, B)], feat[pl.ds(0, B), :], preferred_element_type=F32)
        for b in range(1, 4):
            rows = spread[b, pl.ds(k * B, B)]
            total = total + jnp.dot(rows, feat[pl.ds(b * B, B), :], preferred_element_type=F32)
        term[k] = total
        tsend[k] = term[k, pl.ds((1 - core) * 64, 64), :].astype(BF)
        send(("t", k), tsend.at[k], trecv.at[k], t_send.at[k], t_recv.at[k], sibling)

    def plane_scatter(k):
        arrived(("t", k))
        for a in range(4):
            for b in range(4):
                lanes = pl.ds(b * B, B)
                mine = term[k, pl.ds(core * 64 + a * 16, 16), lanes]
                psend[k, a * 4 + b] = (mine + trecv[k, pl.ds(a * 16, 16), lanes].astype(F32)).astype(BF)
        for o in range(1, 16):
            n = k * 15 + o - 1
            to = plane_peer(o)
            send(("p", k, o), psend.at[k, to["gc"]], precv.at[k, o - 1], p_send.at[n], p_recv.at[n], to)

    def z_exchange(k):
        total = psend[k, gc].astype(F32)
        for o in range(1, 16):
            arrived(("p", k, o))
            total = total + precv[k, o - 1].astype(F32)
        zx[k, z] = total.astype(BF)
        for o in range(1, 8):
            n = k * 7 + o - 1
            send(("x", k, o), zx.at[k, z], zx.at[k, z], x_send.at[n], x_recv.at[n], z_peer(o))

    def plane_gather(k):
        for o in range(1, 8):
            arrived(("x", k, o))
        total = zx[k, 0].astype(F32)
        for a in range(1, 8):
            total = total + zx[k, a].astype(F32)
        wg[k, core, gc] = total.astype(BF)
        for o in range(1, 16):
            n = k * 15 + o - 1
            send(("q", k, o), wg.at[k, core, gc], wg.at[k, core, gc], q_send.at[n], q_recv.at[n], plane_peer(o))

    def core_gather(k):
        for o in range(1, 16):
            arrived(("q", k, o))
        send(("c", k), wg.at[k, core], wg.at[k, core], c_send.at[k], c_recv.at[k], sibling)

    def weight_out(k):
        arrived(("c", k))
        for b in range(4):
            rows = [wg[k, c, a * 4 + b] for c in range(2) for a in range(4)]
            whole = jnp.concatenate(rows, axis=0).astype(F32)
            wg_o[pl.ds(b * B, B), pl.ds(k * B, B)] = whole.T.astype(BF)

    def input_rows(b):
        total = lax.dot_general(spread[b].T, w[...], (((1,), (1,)), ((), ())), preferred_element_type=F32)
        ig_o[pl.ds(b * B, B), :] = total.astype(BF)

    def drain(_):
        for copy in sent:
            copy.wait_send()
        sent.clear()

    def wait_loads():
        for load in loads[2:]:
            load.wait()

    steps = {
        "ring1": first_ring, "pass1": first_forward, "ring2": second_ring, "pass2": second_forward,
        "loads": wait_loads, "mult": multiply, "place": place, "z": z_step, "zend": z_end, "term": weight_term,
        "scatter": plane_scatter, "zsum": z_exchange, "gather": plane_gather, "core": core_gather,
        "out": weight_out, "rows": input_rows, "drain": drain,
    }
    for name, args in plan():
        steps[name](*args)
    drain(0)


def local(out_grad, state, features, weight, block_values, block_rows, block_cols, block_counts):
    values, rows, cols, count = block_values[0, 0], block_rows[0, 0], block_cols[0, 0], block_counts[0, 0]
    slot = jnp.arange(SLOTS, dtype=jnp.int32)
    key = jnp.where(slot < count, cols, 64)
    before = (key[None, :] < key[:, None]) | ((key[None, :] == key[:, None]) & (slot[None, :] < slot[:, None]))
    rank = jnp.sum(before.astype(jnp.int32), axis=1)
    first = jnp.sum(((key[None, :] == key[:, None]) & (slot[None, :] < slot[:, None])).astype(jnp.int32), axis=1) == 0
    device, b = rows // 4, rows % 4
    a0, a1 = device // 4, device % 4
    place = jnp.where(b < 2, a1 * 8 + a0 * 2 + b, 32 + a0 * 8 + a1 * 2 + b - 2)
    word = slot | (place << 8) | (first.astype(jnp.int32) << 16)
    packed = jnp.sum(jnp.where(rank[None, :] == slot[:, None], word[None, :], 0), axis=1)
    column = jnp.arange(64, dtype=jnp.int32)
    upto = jnp.sum((key[None, :] <= column[:, None]).astype(jnp.int32), axis=1)
    here = jnp.sum((key[None, :] == column[:, None]).astype(jnp.int32), axis=1)
    last = jnp.where(here > 0, upto - 1, SLOTS)

    anywhere = pl.BlockSpec(memory_space=pl.ANY)
    dma = pltpu.SemaphoreType.DMA
    grid = (512, 512)
    ig, wg = pl.pallas_call(
        kernel,
        out_shape=(jax.ShapeDtypeStruct(grid, BF), jax.ShapeDtypeStruct(grid, BF)),
        in_specs=[pl.BlockSpec(memory_space=pltpu.SMEM)] * 2 + [anywhere] * 5,
        out_specs=(pl.BlockSpec(memory_space=pltpu.VMEM), pl.BlockSpec(memory_space=pltpu.VMEM)),
        scratch_shapes=[pltpu.VMEM((64, size, B), BF) for _, size in CUTS]
        + [pltpu.VMEM(grid, BF)] * 4
        + [
            pltpu.VMEM((SLOTS, B, B), BF),
            pltpu.VMEM((SLOTS + 1, B, B), BF),
            pltpu.VMEM((B, B), F32),
            pltpu.VMEM((64, 512, B), BF),
            pltpu.VMEM((32, 512, B), BF),
            pltpu.VMEM((8, 4, 512, B), BF),
            pltpu.VMEM((8, 4, 512, B), BF),
            pltpu.VMEM((4, 512, B), BF),
            pltpu.VMEM((UNITS, B, 512), F32),
            pltpu.VMEM((UNITS, 64, 512), BF),
            pltpu.VMEM((UNITS, 64, 512), BF),
            pltpu.VMEM((UNITS, 16, 16, B), BF),
            pltpu.VMEM((UNITS, 15, 16, B), BF),
            pltpu.VMEM((UNITS, 8, 16, B), BF),
            pltpu.VMEM((UNITS, 2, 16, 16, B), BF),
            dma((5,)),
            dma((CHUNKS * 20,)),
            dma((CHUNKS * 20,)),
            dma((CHUNKS * 8,)),
            dma((CHUNKS * 8,)),
            dma((CHUNKS * 14,)),
            dma((CHUNKS * 14,)),
            dma((UNITS,)),
            dma((UNITS,)),
            dma((UNITS * 15,)),
            dma((UNITS * 15,)),
            dma((UNITS * 7,)),
            dma((UNITS * 7,)),
            dma((UNITS * 15,)),
            dma((UNITS * 15,)),
            dma((UNITS,)),
            dma((UNITS,)),
        ],
        compiler_params=pltpu.CompilerParams(
            collective_id=0, has_side_effects=True, vmem_limit_bytes=56 * 1024 * 1024
        ),
        name="graph_backward",
    )(packed, last, out_grad, state, features, weight, values)
    nodes = 512 * lax.axis_size("gr") * lax.axis_size("gc")
    return ig, wg.astype(F32) * nodes ** (-0.5)


def solution(mesh):
    in_specs = (
        P(("gr", "gc"), None),
        P(("gr", "gc"), None),
        P(("gc", "gr"), None),
        P(),
        P("gr", "gc", None, None, None),
        P("gr", "gc", None),
        P("gr", "gc", None),
        P("gr", "gc"),
    )
    out_specs = (P(("gc", "gr"), None), P())
    return jax.shard_map(local, mesh=mesh, in_specs=in_specs, out_specs=out_specs, check_vma=False)
```

```python
import functools

import jax
import jax.numpy as jnp
from jax import lax
from jax.experimental import pallas as pl
from jax.experimental.pallas import tpu as pltpu
from jax.sharding import PartitionSpec as P

MESH = pl.DeviceIdType.MESH
B = 128
SLOTS = 152
CUTS = ((0, 64), (64, 64), (128, 64), (192, 64), (256, 128), (384, 80), (464, 48))
CHUNKS = len(CUTS)
UNITS = 4
UNROLL = 19
BF = jnp.bfloat16
F32 = jnp.float32


GROUPS = ((4, 3, 5), (2, 6), (1, 7, 0))


def plan():
    tasks = {}

    def task(name, args, after=(), needs=(), sends=(), cost=0.1, rank=0.0):
        tasks[name, args] = (tuple(after), tuple(needs), tuple(sends), cost, rank)

    chip, core = 2.4, 0.9
    task("loads", (), cost=1.5, rank=-5)
    for k, (at, size) in enumerate(CUTS):
        unit = size / 2
        task("ring1", (k,), [("ring1", (k - 1,))] if k else [], (), [(("r1", k), "xy", unit, chip)], rank=-9)
        task("pass1", (k,), [], [("r1", k)], [(("f1", k), "xy", unit / 2, chip)], rank=-8)
        before = max(0, k - 1 - (size <= 64))
        gate = [("pass2", (before,))] if k > 1 else []
        task(
            "ring2", (k,), gate + ([("ring2", (k - 1,))] if k else []), [("f1", k)],
            [(("a", k), "xy", unit * 2, chip), (("b", k), "xy", unit * 2, chip)], rank=-7,
        )
        task("pass2", (k,), [], [("a", k)], [(("f2", k), "xy", unit * 2, chip)], rank=-8)
        load = 0.5 + size / 128
        follow = [("place", (k - 1, GROUPS[-1]))] if k else [("loads", ())]
        task("mult", (k, 0), follow, [("b", k), ("f2", k)], cost=load, rank=k)
        task("mult", (k, 1), [("mult", (k, 0))], cost=load, rank=k)
        for i, group in enumerate(GROUPS):
            task(
                "place", (k, group), [("place", (k, GROUPS[i - 1])) if i else ("mult", (k, 1))], (),
                [(("e", k, d), "core", size, core) for d in group], 0.08 * len(group), k - 0.5,
            )
        for chain in range(2):
            for t in range(4 - chain, 0, -1):
                needs = [("e", k, d) for d in sorted({t, 8 - t})]
                if t < 4 - chain:
                    needs.append(("z", k, chain, t + 1))
                task("z", (k, chain, t), (), needs, [(("z", k, chain, t), "z", size / 2, chip)], 0.2, -6 + k / 10)
        task("zend", (k,), (), [("e", k, 0), ("z", k, 0, 1), ("z", k, 1, 1)], cost=0.25, rank=-5 + k / 10)
    for u in range(UNITS):
        ends = [("zend", (k,)) for k, (at, _) in enumerate(CUTS) if at // B == u]
        task("term", (u,), ends, (), [(("t", u), "core", 64, core)], 0.7, u - 1)
        task("scatter", (u,), (), [("t", u)], [(("p", u), "xy", 32, 4.5)], 0.5, u - 1)
        behind = [("z", (CHUNKS - 1, 0, 1))] if u < UNITS - 1 else []
        task("zsum", (u,), behind, [("p", u)], [(("x", u), "z", 32, 4.5)], 0.4, u - 1)
        task("gather", (u,), (), [("x", u)], [(("q", u), "xy", 32, 4.5)], 0.5, u - 1)
        task("core", (u,), (), [("q", u)], [(("c", u), "core", 64, core)], 0.2, u - 1)
        task("out", (u,), (), [("c", u)], cost=0.4, rank=u + 1)
    for b in range(4):
        task("rows", (b,), [("zend", (CHUNKS - 1,)), ("scatter", (UNITS - 1,))], cost=0.6, rank=20)
    sums = [("z", (k, chain, 1)) for k in range(CHUNKS) for chain in range(2)]
    task("drain", (0,), [*sums, ("scatter", (UNITS - 1,))], cost=1.0, rank=30)
    task("drain", (1,), [("gather", (u,)) for u in range(UNITS)], cost=0.5, rank=30)

    now, free, come, done, order = 0.0, {"xy": 0.0, "z": 0.0, "core": 0.0}, {}, set(), []
    rate = {"xy": 48.0, "z": 48.0, "core": 600.0}
    while tasks:
        best = None
        for key, (after, needs, _, cost, rank) in tasks.items():
            if all(a in done for a in after) and all(n in come for n in needs):
                ready = max([now] + [come[n] for n in needs])
                score = (ready, rank)
                if best is None or score < best[0]:
                    best = (score, key)
        (now, _), key = best
        _, _, sends, cost, _ = tasks.pop(key)
        now += cost
        for message, link, kib, latency in sends:
            free[link] = max(free[link], now) + kib / rate[link]
            come[message] = free[link] + latency
        done.add(key)
        order.append(key)
    return order


def kernel(
    count, row_ids, col_ids, og_h, pre_h, feat_h, w_h, vals_h,
    ig_o, wg_o,
    g0, g1, g2, g3, g4, g5, g6, ids, table, lists, og, pre, feat, w, vals, prods, carry, part, sib, zs, zr, spread, term, tsend, trecv,
    psend, precv, zx, wg,
    local_sem, g_send, g_recv, e_send, e_recv, z_send, z_recv, t_send, t_recv, p_send, p_recv,
    x_send, x_recv, q_send, q_recv, c_send, c_recv,
):
    gathered = (g0, g1, g2, g3, g4, g5, g6)
    gr, gc = lax.axis_index("gr"), lax.axis_index("gc")
    scale = (512 * lax.axis_size("gr") * lax.axis_size("gc")) ** (-0.5)
    z, core = gr // 2, gr % 2
    x, y = gc // 4, gc % 4
    sibling = {"gr": z * 2 + (1 - core), "gc": gc}

    def z_peer(d):
        return {"gr": ((z + d) % 8) * 2 + core, "gc": gc}

    def plane_peer(d):
        return {"gr": gr, "gc": (gc + d) % 16}

    def x_peer(d):
        return {"gr": gr, "gc": ((x + d + 4) % 4) * 4 + y}

    def y_peer(d):
        return {"gr": gr, "gc": x * 4 + (y + d + 4) % 4}

    loads = [
        pltpu.make_async_copy(og_h, og, local_sem.at[0]),
        pltpu.make_async_copy(pre_h, pre, local_sem.at[1]),
        pltpu.make_async_copy(vals_h, vals, local_sem.at[2]),
        pltpu.make_async_copy(feat_h, feat, local_sem.at[3]),
        pltpu.make_async_copy(w_h, w, local_sem.at[4]),
    ]
    for load in loads:
        load.start()

    barrier = pltpu.get_barrier_semaphore()
    pl.semaphore_signal(barrier, inc=1, device_id=sibling, device_id_type=MESH)

    for device in (z_peer(1), z_peer(7), x_peer(1), x_peer(-1), y_peer(1), y_peer(-1)):
        pl.semaphore_signal(barrier, inc=1, device_id=device, device_id_type=MESH)

    ring = (x, y)
    cross = (y, x)
    near = (x_peer, y_peer)
    far = (y_peer, x_peer)

    def unit(h, p, q):
        return h * 32 + p * 8 + q * 2

    loads[0].wait()
    loads[1].wait()
    for k in range(UNITS):
        for b in range(4):
            rows, cols = pl.ds(b * B, B), pl.ds(k * B, B)
            block = og[rows, cols]
            block = jnp.where(pre[rows, cols].astype(F32) > 0, block.astype(F32), 0.0).T.astype(BF)
            h = b // 2
            for n, (at, size) in enumerate(CUTS):
                if at // B == k:
                    gathered[n][unit(h, cross[h], ring[h]) + b % 2] = block[at % B : at % B + size]
    prods[SLOTS] = jnp.zeros((B, B), BF)
    pl.semaphore_wait(barrier, 7)

    def send(src, dst, send_sem, recv_sem, device):
        pltpu.make_async_remote_copy(
            src_ref=src, dst_ref=dst, send_sem=send_sem, recv_sem=recv_sem, device_id=device, device_id_type=MESH
        ).start()

    def bytes_of(ref, sem):
        return pltpu.make_async_remote_copy(
            src_ref=ref, dst_ref=ref, send_sem=sem, recv_sem=sem, device_id=sibling, device_id_type=MESH
        )

    def arrived(ref, sem):
        bytes_of(ref, sem).wait_recv()

    def left(ref, sem):
        bytes_of(ref, sem).wait_send()

    def gather_copy(stage, k, h, d, at, size, device):
        where = gathered[k].at[pl.ds(at, size)]
        send(where, where, g_send.at[k], g_recv.at[k * 4 + min(stage, 3)], device)

    def gather_arrived(k, stage, blocks):
        arrived(gathered[k].at[pl.ds(0, blocks)], g_recv.at[k * 4 + stage])

    def first_ring(k):
        for h in range(2):
            for d in (1, -1):
                gather_copy(0, k, h, d, unit(h, cross[h], ring[h]), 2, near[h](d))

    def first_forward(k):
        gather_arrived(k, 0, 8)
        for h in range(2):
            for d in (1, -1):
                came = (ring[h] - d + 4) % 4
                gather_copy(1, k, h, d, unit(h, cross[h], came) + (0 if d == 1 else 1), 1, near[h](d))

    def second_ring(k):
        gather_arrived(k, 1, 4)
        for part_no in range(2):
            for h in range(2):
                for d in (1, -1):
                    which = part_no if d == 1 else 1 - part_no
                    gather_copy(2 + part_no, k, h, d, unit(h, cross[h], 0) + 4 * which, 4, far[h](d))

    def second_forward(k):
        gather_arrived(k, 2, 16)
        for h in range(2):
            for d in (1, -1):
                came = (cross[h] - d + 4) % 4
                gather_copy(4, k, h, d, unit(h, came, 0) + (0 if d == 1 else 4), 4, far[h](d))

    def multiply(k, half):
        at, size = CUTS[k]
        source = gathered[k]
        if half == 0:
            gather_arrived(k, 3, 32)

        def some(t, total):
            for u in range(UNROLL):
                s = (half * 4 + t) * UNROLL + u
                word = lists[0, s]
                term_now = jnp.dot(source[(word >> 8) & 255], vals[word & 255], preferred_element_type=F32)
                total = jnp.where((word >> 16) != 0, term_now, total + term_now)
                prods[s, pl.ds(0, size)] = total.astype(BF)
            return total

        begin = jnp.zeros((size, B), F32) if half == 0 else carry[pl.ds(0, size), :]
        total = lax.fori_loop(0, SLOTS // UNROLL // 2, some, begin)
        if half == 0:
            carry[pl.ds(0, size), :] = total

    def place(k, group):
        at, size = CUTS[k]
        for d in group:
            zp = (z + d) % 8

            def one(j, _):
                part[zp * 8 + j, pl.ds(at, size)] = prods[lists[1, zp * 8 + j], pl.ds(0, size)]
                return 0

            lax.fori_loop(0, 8, one, 0, unroll=True)
            n = k * len(GROUPS) + GROUPS.index(group)
            send(
                part.at[pl.ds(zp * 8 + (1 - core) * 4, 4), pl.ds(at, size)],
                sib.at[pl.ds(zp * 4, 4), pl.ds(at, size)],
                e_send.at[k], e_recv.at[n], sibling,
            )

    exchanged = set()

    def own(k, d, b):
        group = next(n for n, members in enumerate(GROUPS) if d in members)
        if (k, group) not in exchanged:
            exchanged.add((k, group))
            arrived(sib.at[pl.ds(0, 4 * len(GROUPS[group])), pl.ds(*CUTS[k])], e_recv.at[k * len(GROUPS) + group])
        zp = (z + d) % 8
        cut = pl.ds(*CUTS[k])
        return part[zp * 8 + core * 4 + b, cut].astype(F32) + sib[zp * 4 + b, cut].astype(F32)

    def z_sem(k, chain, t):
        return z_recv.at[k * 7 + (t + 2 if chain == 0 else t - 1)]

    def z_step(k, chain, t):
        cut = pl.ds(*CUTS[k])
        fresh = t == 4 - chain
        if not fresh:
            arrived(zr.at[0, :, cut], z_sem(k, chain, t + 1))
        for side in range(2):
            h = side if chain == 0 else 1 - side
            d = 8 - t if side == 0 else t
            n = side * 4 + t - 1
            for b in (2 * h, 2 * h + 1):
                value = own(k, d, b)
                if not fresh:
                    value = value + zr[n + 1, b, cut].astype(F32)
                zs[n, b, cut] = value.astype(BF)
            blocks = pl.ds(2 * h, 2)
            send(
                zs.at[n, blocks, cut], zr.at[n, blocks, cut],
                z_send.at[k], z_sem(k, chain, t), z_peer(7 if side == 0 else 1),
            )

    def z_end(k):
        cut = pl.ds(*CUTS[k])
        for chain in range(2):
            arrived(zr.at[0, :, cut], z_sem(k, chain, 1))
        for b in range(4):
            total = own(k, 0, b) + zr[0, b, cut].astype(F32) + zr[4, b, cut].astype(F32)
            spread[b, cut] = total.astype(BF)

    def weight_term(k):
        total = jnp.dot(spread[0, pl.ds(k * B, B)], feat[pl.ds(0, B), :], preferred_element_type=F32)
        for b in range(1, 4):
            rows = spread[b, pl.ds(k * B, B)]
            total = total + jnp.dot(rows, feat[pl.ds(b * B, B), :], preferred_element_type=F32)
        term[k] = total
        tsend[k] = term[k, pl.ds((1 - core) * 64, 64), :].astype(BF)
        send(tsend.at[k], trecv.at[k], t_send.at[k], t_recv.at[k], sibling)

    def plane_scatter(k):
        arrived(trecv.at[k], t_recv.at[k])
        for a in range(4):
            for b in range(4):
                lanes = pl.ds(b * B, B)
                mine = term[k, pl.ds(core * 64 + a * 16, 16), lanes]
                psend[k, a * 4 + b] = (mine + trecv[k, pl.ds(a * 16, 16), lanes].astype(F32)).astype(BF)
        for o in range(1, 16):
            to = plane_peer(o)
            send(psend.at[k, to["gc"]], precv.at[k, o - 1], p_send.at[k], p_recv.at[k], to)

    def z_exchange(k):
        arrived(precv.at[k], p_recv.at[k])
        total = psend[k, gc].astype(F32)
        for o in range(1, 16):
            total = total + precv[k, o - 1].astype(F32)
        zx[k, z] = total.astype(BF)
        for o in range(1, 8):
            send(zx.at[k, z], zx.at[k, z], x_send.at[k], x_recv.at[k], z_peer(o))

    def plane_gather(k):
        arrived(zx.at[k, pl.ds(0, 7)], x_recv.at[k])
        total = zx[k, 0].astype(F32)
        for a in range(1, 8):
            total = total + zx[k, a].astype(F32)
        wg[k, core, gc] = total.astype(BF)
        for o in range(1, 16):
            send(wg.at[k, core, gc], wg.at[k, core, gc], q_send.at[k], q_recv.at[k], plane_peer(o))

    def core_gather(k):
        arrived(wg.at[k, core, pl.ds(0, 15)], q_recv.at[k])
        send(wg.at[k, core], wg.at[k, core], c_send.at[k], c_recv.at[k], sibling)

    def weight_out(k):
        arrived(wg.at[k, core], c_recv.at[k])
        for b in range(4):
            rows = [wg[k, c, a * 4 + b] for c in range(2) for a in range(4)]
            whole = jnp.concatenate(rows, axis=0).astype(F32)
            wg_o[pl.ds(b * B, B), pl.ds(k * B, B)] = whole.T * scale

    def input_rows(b):
        total = lax.dot_general(spread[b].T, w[...], (((1,), (1,)), ((), ())), preferred_element_type=F32)
        ig_o[pl.ds(b * B, B), :] = total.astype(BF)

    def drain(stage):
        if stage == 0:
            for k in range(CHUNKS):
                cut = pl.ds(*CUTS[k])
                left(gathered[k].at[pl.ds(0, 60)], g_send.at[k])
                left(sib.at[:, cut], e_send.at[k])
                left(zs.at[pl.ds(0, 7), :, cut], z_send.at[k])
            return
        for u in range(UNITS):
            if stage == 1:
                left(tsend.at[u], t_send.at[u])
                left(precv.at[u], p_send.at[u])
                left(zx.at[u, pl.ds(0, 7)], x_send.at[u])
            else:
                left(precv.at[u], q_send.at[u])
                left(wg.at[u, core], c_send.at[u])

    def wait_loads():
        ids[...] = jnp.zeros((8, 256), jnp.int32)
        ids[0:1, 0:SLOTS] = row_ids[0]
        ids[1:2, 0:SLOTS] = col_ids[0]
        slot, row = lax.broadcasted_iota(jnp.int32, (1, 256), 1), ids[0:1, :]
        quarter, device = row & 3, row >> 2
        a0, a1 = device >> 2, device & 3
        where = jnp.where(quarter < 2, a1 * 8 + a0 * 2 + quarter, 32 + a0 * 8 + a1 * 2 + quarter - 2)
        key = jnp.where(slot < count[0, 0], ids[1:2, :], 64)
        across, down = (lax.broadcasted_iota(jnp.int32, (256, 256), n) for n in (1, 0))
        key_across = jnp.broadcast_to(key, (256, 256))
        key_down = key_across.T
        word_down = jnp.broadcast_to(slot | (where << 8), (256, 256)).T
        same = (key_across == key_down) & (across < down)
        less = (key_across < key_down) | same
        rank = jnp.sum(less.astype(jnp.int32), axis=1, keepdims=True)
        opens = jnp.sum(same.astype(jnp.int32), axis=1, keepdims=True) == 0
        word_down = word_down | (opens.astype(jnp.int32) << 16)
        upto = jnp.sum((key_down <= across).astype(jnp.int32), axis=0, keepdims=True)
        here = jnp.sum((key_down == across).astype(jnp.int32), axis=0, keepdims=True)
        table[...] = jnp.zeros((8, 256), jnp.int32)
        table[0:1, :] = jnp.sum(jnp.where(rank == across, word_down, 0), axis=0, keepdims=True)
        table[1:2, :] = jnp.where(here > 0, upto - 1, SLOTS)
        pltpu.sync_copy(table, lists)
        for load in loads[2:]:
            load.wait()

    steps = {
        "ring1": first_ring, "pass1": first_forward, "ring2": second_ring, "pass2": second_forward,
        "loads": wait_loads, "mult": multiply, "place": place, "z": z_step, "zend": z_end, "term": weight_term,
        "scatter": plane_scatter, "zsum": z_exchange, "gather": plane_gather, "core": core_gather,
        "out": weight_out, "rows": input_rows, "drain": drain,
    }
    for name, args in plan():
        steps[name](*args)
    drain(2)


def finish(ig, wg, ig_o, wg_o):
    ig_o[...] = ig[...]
    wg_o[...] = wg[...]


def local(out_grad, state, features, weight, block_values, block_rows, block_cols, block_counts):
    anywhere = pl.BlockSpec(memory_space=pl.ANY)
    dma = pltpu.SemaphoreType.DMA
    grid = (512, 512)
    ig, wg = pl.pallas_call(
        kernel,
        out_shape=(jax.ShapeDtypeStruct(grid, BF), jax.ShapeDtypeStruct(grid, F32)),
        in_specs=[pl.BlockSpec(memory_space=pltpu.SMEM)] + [pl.BlockSpec(memory_space=pltpu.VMEM)] * 2 + [anywhere] * 5,
        out_specs=(pl.BlockSpec(memory_space=pltpu.VMEM), pl.BlockSpec(memory_space=pltpu.VMEM)),
        scratch_shapes=[pltpu.VMEM((64, size, B), BF) for _, size in CUTS]
        + [pltpu.VMEM((8, 256), jnp.int32)] * 2
        + [pltpu.SMEM((8, 256), jnp.int32)]
        + [pltpu.VMEM(grid, BF)] * 4
        + [
            pltpu.VMEM((SLOTS, B, B), BF),
            pltpu.VMEM((SLOTS + 1, B, B), BF),
            pltpu.VMEM((B, B), F32),
            pltpu.VMEM((64, 512, B), BF),
            pltpu.VMEM((32, 512, B), BF),
            pltpu.VMEM((8, 4, 512, B), BF),
            pltpu.VMEM((8, 4, 512, B), BF),
            pltpu.VMEM((4, 512, B), BF),
            pltpu.VMEM((UNITS, B, 512), F32),
            pltpu.VMEM((UNITS, 64, 512), BF),
            pltpu.VMEM((UNITS, 64, 512), BF),
            pltpu.VMEM((UNITS, 16, 16, B), BF),
            pltpu.VMEM((UNITS, 15, 16, B), BF),
            pltpu.VMEM((UNITS, 8, 16, B), BF),
            pltpu.VMEM((UNITS, 2, 16, 16, B), BF),
            dma((5,)),
            dma((CHUNKS,)),
            dma((CHUNKS * 4,)),
            dma((CHUNKS,)),
            dma((CHUNKS * len(GROUPS),)),
            dma((CHUNKS,)),
            dma((CHUNKS * 7,)),
        ]
        + [dma((UNITS,))] * 10,
        compiler_params=pltpu.CompilerParams(
            collective_id=0, has_side_effects=True, vmem_limit_bytes=56 * 1024 * 1024
        ),
        name="graph_backward",
    )(block_counts, block_rows, block_cols, out_grad, state, features, weight, block_values[0, 0])
    return pl.pallas_call(
        finish,
        out_shape=(jax.ShapeDtypeStruct(grid, BF), jax.ShapeDtypeStruct(grid, F32)),
        name="finish",
    )(ig, wg)


def solution(mesh):
    in_specs = (
        P(("gr", "gc"), None),
        P(("gr", "gc"), None),
        P(("gc", "gr"), None),
        P(),
        P("gr", "gc", None, None, None),
        P("gr", "gc", None),
        P("gr", "gc", None),
        P("gr", "gc"),
    )
    out_specs = (P(("gc", "gr"), None), P())
    return jax.shard_map(local, mesh=mesh, in_specs=in_specs, out_specs=out_specs, check_vma=False)
```

```python
import functools

import jax
import jax.numpy as jnp
from jax import lax
from jax.experimental import pallas as pl
from jax.experimental.pallas import tpu as pltpu
from jax.sharding import PartitionSpec as P

MESH = pl.DeviceIdType.MESH
B = 128
SLOTS = 152
CUTS = ((0, 64), (64, 64), (128, 64), (192, 64), (256, 64), (320, 64), (384, 128))
CHUNKS = len(CUTS)
UNITS = 4
UNROLL = 38
BF = jnp.bfloat16
F32 = jnp.float32


GROUPS = ((4, 3, 5), (2, 6), (1, 7, 0))


def plan():
    tasks = {}

    def task(name, args, after=(), needs=(), sends=(), cost=0.1, rank=0.0):
        tasks[name, args] = (tuple(after), tuple(needs), tuple(sends), cost, rank)

    chip, core = 2.4, 0.9
    task("loads", (), cost=1.2, rank=-5)
    for k, (at, size) in enumerate(CUTS):
        unit = size / 2
        task("ring1", (k,), [("ring1", (k - 1,))] if k else [], (), [(("r1", k), "xy", unit, chip)], rank=-9)
        task("pass1", (k,), [], [("r1", k)], [(("f1", k), "xy", unit / 2, chip)], rank=-8)
        before = max(0, k - 1 - (size <= 64))
        gate = [("pass2", (before,))] if k > 1 else []
        task(
            "ring2", (k,), gate + ([("ring2", (k - 1,))] if k else []), [("f1", k)],
            [(("a", k), "xy", unit * 2, chip), (("b", k), "xy", unit * 2, chip)], rank=-7,
        )
        task("pass2", (k,), [], [("a", k)], [(("f2", k), "xy", unit * 2, chip)], rank=-8)
        load = 0.95
        follow = [("place", (k - 1, GROUPS[-1]))] if k else [("loads", ())]
        task("mult", (k, 0), follow, [("b", k), ("f2", k)], cost=load, rank=k)
        task("mult", (k, 1), [("mult", (k, 0))], cost=load, rank=k)
        for i, group in enumerate(GROUPS):
            task(
                "place", (k, group), [("place", (k, GROUPS[i - 1])) if i else ("mult", (k, 1))], (),
                [(("e", k, d), "core", size, core) for d in group], 0.08 * len(group), k - 0.5,
            )
        for chain in range(2):
            for t in range(4 - chain, 0, -1):
                needs = [("e", k, d) for d in sorted({t, 8 - t})]
                if t < 4 - chain:
                    needs.append(("z", k, chain, t + 1))
                task("z", (k, chain, t), (), needs, [(("z", k, chain, t), "z", size / 2, chip)], 0.2, -6 + k / 10)
        task("zend", (k,), (), [("e", k, 0), ("z", k, 0, 1), ("z", k, 1, 1)], cost=0.25, rank=-5 + k / 10)
    for u in range(UNITS):
        ends = [("zend", (k,)) for k, (at, _) in enumerate(CUTS) if at // B == u]
        task("term", (u,), ends, (), [(("t", u), "core", 64, core)], 0.7, u - 1)
        task("scatter", (u,), (), [("t", u)], [(("p", u), "xy", 32, 4.5)], 0.5, u - 1)
        behind = [("z", (CHUNKS - 1, 0, 1))] if u < UNITS - 1 else []
        task("zsum", (u,), behind, [("p", u)], [(("x", u), "z", 32, 4.5)], 0.4, u - 1)
        task("gather", (u,), (), [("x", u)], [(("q", u), "xy", 32, 4.5)], 0.5, u - 1)
        task("core", (u,), (), [("q", u)], [(("c", u), "core", 64, core)], 0.2, u - 1)
        task("out", (u,), (), [("c", u)], cost=0.4, rank=u + 1)
    for b in range(4):
        task("rows", (b,), [("zend", (CHUNKS - 1,)), ("scatter", (UNITS - 1,))], cost=0.6, rank=20)
    sums = [("z", (k, chain, 1)) for k in range(CHUNKS) for chain in range(2)]
    task("drain", (0,), [*sums, ("scatter", (UNITS - 1,))], cost=1.0, rank=30)
    task("drain", (1,), [("gather", (u,)) for u in range(UNITS)], cost=0.5, rank=30)

    now, free, come, done, order = 0.0, {"xy": 0.0, "z": 0.0, "core": 0.0}, {}, set(), []
    rate = {"xy": 48.0, "z": 48.0, "core": 600.0}
    while tasks:
        best = None
        for key, (after, needs, _, cost, rank) in tasks.items():
            if all(a in done for a in after) and all(n in come for n in needs):
                ready = max([now] + [come[n] for n in needs])
                score = (ready, rank)
                if best is None or score < best[0]:
                    best = (score, key)
        (now, _), key = best
        _, _, sends, cost, _ = tasks.pop(key)
        now += cost
        for message, link, kib, latency in sends:
            free[link] = max(free[link], now) + kib / rate[link]
            come[message] = free[link] + latency
        done.add(key)
        order.append(key)
    return order


def kernel(
    count, row_ids, col_ids, og_h, pre_h, feat_h, w_h, vals_h,
    ig_o, wg_o,
    g0, g1, g2, g3, g4, g5, g6, ids, table, lists, og, pre, feat, w, vals, prods, carry, part, sib, zs, zr, spread, term, tsend, trecv,
    psend, precv, zx, wg,
    local_sem, g_send, g_recv, e_send, e_recv, z_send, z_recv, t_send, t_recv, p_send, p_recv,
    x_send, x_recv, q_send, q_recv, c_send, c_recv,
):
    gathered = (g0, g1, g2, g3, g4, g5, g6)
    gr, gc = lax.axis_index("gr"), lax.axis_index("gc")
    scale = (512 * lax.axis_size("gr") * lax.axis_size("gc")) ** (-0.5)
    z, core = gr // 2, gr % 2
    x, y = gc // 4, gc % 4
    sibling = {"gr": z * 2 + (1 - core), "gc": gc}

    def z_peer(d):
        return {"gr": ((z + d) % 8) * 2 + core, "gc": gc}

    def plane_peer(d):
        return {"gr": gr, "gc": (gc + d) % 16}

    def x_peer(d):
        return {"gr": gr, "gc": ((x + d + 4) % 4) * 4 + y}

    def y_peer(d):
        return {"gr": gr, "gc": x * 4 + (y + d + 4) % 4}

    loads = [
        pltpu.make_async_copy(og_h, og, local_sem.at[0]),
        pltpu.make_async_copy(pre_h, pre, local_sem.at[1]),
        pltpu.make_async_copy(vals_h, vals, local_sem.at[2]),
        pltpu.make_async_copy(feat_h, feat, local_sem.at[3]),
        pltpu.make_async_copy(w_h, w, local_sem.at[4]),
    ]
    for load in loads:
        load.start()

    barrier = pltpu.get_barrier_semaphore()
    pl.semaphore_signal(barrier, inc=1, device_id=sibling, device_id_type=MESH)

    for device in (z_peer(1), z_peer(7), x_peer(1), x_peer(-1), y_peer(1), y_peer(-1)):
        pl.semaphore_signal(barrier, inc=1, device_id=device, device_id_type=MESH)

    ring = (x, y)
    cross = (y, x)
    near = (x_peer, y_peer)
    far = (y_peer, x_peer)

    def unit(h, p, q):
        return h * 32 + p * 8 + q * 2

    loads[0].wait()
    loads[1].wait()
    for k in range(UNITS):
        for b in range(4):
            rows, cols = pl.ds(b * B, B), pl.ds(k * B, B)
            block = og[rows, cols]
            block = jnp.where(pre[rows, cols].astype(F32) > 0, block.astype(F32), 0.0).T.astype(BF)
            h = b // 2
            for n, (at, size) in enumerate(CUTS):
                if at // B == k:
                    gathered[n][unit(h, cross[h], ring[h]) + b % 2] = block[at % B : at % B + size]
    prods[SLOTS] = jnp.zeros((B, B), BF)
    pl.semaphore_wait(barrier, 7)

    def send(src, dst, send_sem, recv_sem, device):
        pltpu.make_async_remote_copy(
            src_ref=src, dst_ref=dst, send_sem=send_sem, recv_sem=recv_sem, device_id=device, device_id_type=MESH
        ).start()

    def bytes_of(ref, sem):
        return pltpu.make_async_remote_copy(
            src_ref=ref, dst_ref=ref, send_sem=sem, recv_sem=sem, device_id=sibling, device_id_type=MESH
        )

    def arrived(ref, sem):
        bytes_of(ref, sem).wait_recv()

    def left(ref, sem):
        bytes_of(ref, sem).wait_send()

    def gather_copy(stage, k, h, d, at, size, device):
        where = gathered[k].at[pl.ds(at, size)]
        send(where, where, g_send.at[k], g_recv.at[k * 4 + min(stage, 3)], device)

    def gather_arrived(k, stage, blocks):
        arrived(gathered[k].at[pl.ds(0, blocks)], g_recv.at[k * 4 + stage])

    def first_ring(k):
        for h in range(2):
            for d in (1, -1):
                gather_copy(0, k, h, d, unit(h, cross[h], ring[h]), 2, near[h](d))

    def first_forward(k):
        gather_arrived(k, 0, 8)
        for h in range(2):
            for d in (1, -1):
                came = (ring[h] - d + 4) % 4
                gather_copy(1, k, h, d, unit(h, cross[h], came) + (0 if d == 1 else 1), 1, near[h](d))

    def second_ring(k):
        gather_arrived(k, 1, 4)
        for part_no in range(2):
            for h in range(2):
                for d in (1, -1):
                    which = part_no if d == 1 else 1 - part_no
                    gather_copy(2 + part_no, k, h, d, unit(h, cross[h], 0) + 4 * which, 4, far[h](d))

    def second_forward(k):
        gather_arrived(k, 2, 16)
        for h in range(2):
            for d in (1, -1):
                came = (cross[h] - d + 4) % 4
                gather_copy(4, k, h, d, unit(h, came, 0) + (0 if d == 1 else 4), 4, far[h](d))

    def multiply(k, half):
        at, size = CUTS[k]
        source = gathered[k]
        if half == 0:
            gather_arrived(k, 3, 32)

        def some(t, total):
            for u in range(UNROLL):
                s = (half * 2 + t) * UNROLL + u
                word = lists[0, s]
                term_now = jnp.dot(source[(word >> 8) & 255], vals[word & 255], preferred_element_type=F32)
                total = jnp.where((word >> 16) != 0, term_now, total + term_now)
                prods[s, pl.ds(0, size)] = total.astype(BF)
            return total

        begin = jnp.zeros((size, B), F32) if half == 0 else carry[pl.ds(0, size), :]
        total = lax.fori_loop(0, SLOTS // UNROLL // 2, some, begin)
        if half == 0:
            carry[pl.ds(0, size), :] = total

    def place(k, group):
        at, size = CUTS[k]
        for d in group:
            zp = (z + d) % 8

            def one(j, _):
                part[zp * 8 + j, pl.ds(at, size)] = prods[lists[1, zp * 8 + j], pl.ds(0, size)]
                return 0

            lax.fori_loop(0, 8, one, 0, unroll=True)
            n = k * len(GROUPS) + GROUPS.index(group)
            send(
                part.at[pl.ds(zp * 8 + (1 - core) * 4, 4), pl.ds(at, size)],
                sib.at[pl.ds(zp * 4, 4), pl.ds(at, size)],
                e_send.at[k], e_recv.at[n], sibling,
            )

    exchanged = set()

    def own(k, d, b):
        group = next(n for n, members in enumerate(GROUPS) if d in members)
        if (k, group) not in exchanged:
            exchanged.add((k, group))
            arrived(sib.at[pl.ds(0, 4 * len(GROUPS[group])), pl.ds(*CUTS[k])], e_recv.at[k * len(GROUPS) + group])
        zp = (z + d) % 8
        cut = pl.ds(*CUTS[k])
        return part[zp * 8 + core * 4 + b, cut].astype(F32) + sib[zp * 4 + b, cut].astype(F32)

    def z_sem(k, chain, t):
        return z_recv.at[k * 7 + (t + 2 if chain == 0 else t - 1)]

    def z_step(k, chain, t):
        cut = pl.ds(*CUTS[k])
        fresh = t == 4 - chain
        if not fresh:
            arrived(zr.at[0, :, cut], z_sem(k, chain, t + 1))
        for side in range(2):
            h = side if chain == 0 else 1 - side
            d = 8 - t if side == 0 else t
            n = side * 4 + t - 1
            for b in (2 * h, 2 * h + 1):
                value = own(k, d, b)
                if not fresh:
                    value = value + zr[n + 1, b, cut].astype(F32)
                zs[n, b, cut] = value.astype(BF)
            blocks = pl.ds(2 * h, 2)
            send(
                zs.at[n, blocks, cut], zr.at[n, blocks, cut],
                z_send.at[k], z_sem(k, chain, t), z_peer(7 if side == 0 else 1),
            )

    def z_end(k):
        cut = pl.ds(*CUTS[k])
        for chain in range(2):
            arrived(zr.at[0, :, cut], z_sem(k, chain, 1))
        for b in range(4):
            total = own(k, 0, b) + zr[0, b, cut].astype(F32) + zr[4, b, cut].astype(F32)
            spread[b, cut] = total.astype(BF)

    def weight_term(k):
        total = jnp.dot(spread[0, pl.ds(k * B, B)], feat[pl.ds(0, B), :], preferred_element_type=F32)
        for b in range(1, 4):
            rows = spread[b, pl.ds(k * B, B)]
            total = total + jnp.dot(rows, feat[pl.ds(b * B, B), :], preferred_element_type=F32)
        term[k] = total
        tsend[k] = term[k, pl.ds((1 - core) * 64, 64), :].astype(BF)
        send(tsend.at[k], trecv.at[k], t_send.at[k], t_recv.at[k], sibling)

    def plane_scatter(k):
        arrived(trecv.at[k], t_recv.at[k])
        for a in range(4):
            for b in range(4):
                lanes = pl.ds(b * B, B)
                mine = term[k, pl.ds(core * 64 + a * 16, 16), lanes]
                psend[k, a * 4 + b] = (mine + trecv[k, pl.ds(a * 16, 16), lanes].astype(F32)).astype(BF)
        for o in range(1, 16):
            to = plane_peer(o)
            send(psend.at[k, to["gc"]], precv.at[k, o - 1], p_send.at[k], p_recv.at[k], to)

    def z_exchange(k):
        arrived(precv.at[k], p_recv.at[k])
        total = psend[k, gc].astype(F32)
        for o in range(1, 16):
            total = total + precv[k, o - 1].astype(F32)
        zx[k, z] = total.astype(BF)
        for o in range(1, 8):
            send(zx.at[k, z], zx.at[k, z], x_send.at[k], x_recv.at[k], z_peer(o))

    def plane_gather(k):
        arrived(zx.at[k, pl.ds(0, 7)], x_recv.at[k])
        total = zx[k, 0].astype(F32)
        for a in range(1, 8):
            total = total + zx[k, a].astype(F32)
        wg[k, core, gc] = total.astype(BF)
        for o in range(1, 16):
            send(wg.at[k, core, gc], wg.at[k, core, gc], q_send.at[k], q_recv.at[k], plane_peer(o))

    def core_gather(k):
        arrived(wg.at[k, core, pl.ds(0, 15)], q_recv.at[k])
        send(wg.at[k, core], wg.at[k, core], c_send.at[k], c_recv.at[k], sibling)

    def weight_out(k):
        arrived(wg.at[k, core], c_recv.at[k])
        for b in range(4):
            rows = [wg[k, c, a * 4 + b] for c in range(2) for a in range(4)]
            whole = jnp.concatenate(rows, axis=0).astype(F32)
            wg_o[pl.ds(b * B, B), pl.ds(k * B, B)] = whole.T * scale

    def input_rows(b):
        total = lax.dot_general(spread[b].T, w[...], (((1,), (1,)), ((), ())), preferred_element_type=F32)
        ig_o[pl.ds(b * B, B), :] = total.astype(BF)

    def drain(stage):
        if stage == 0:
            for k in range(CHUNKS):
                cut = pl.ds(*CUTS[k])
                left(gathered[k].at[pl.ds(0, 60)], g_send.at[k])
                left(sib.at[:, cut], e_send.at[k])
                left(zs.at[pl.ds(0, 7), :, cut], z_send.at[k])
            return
        for u in range(UNITS):
            if stage == 1:
                left(tsend.at[u], t_send.at[u])
                left(precv.at[u], p_send.at[u])
                left(zx.at[u, pl.ds(0, 7)], x_send.at[u])
            else:
                left(precv.at[u], q_send.at[u])
                left(wg.at[u, core], c_send.at[u])

    def wait_loads():
        ids[...] = jnp.zeros((8, 256), jnp.int32)
        ids[0:1, 0:SLOTS] = row_ids[0]
        ids[1:2, 0:SLOTS] = col_ids[0]
        slot, row = lax.broadcasted_iota(jnp.int32, (1, 256), 1), ids[0:1, :]
        quarter, device = row & 3, row >> 2
        a0, a1 = device >> 2, device & 3
        where = jnp.where(quarter < 2, a1 * 8 + a0 * 2 + quarter, 32 + a0 * 8 + a1 * 2 + quarter - 2)
        key = jnp.where(slot < count[0, 0], ids[1:2, :], 64)
        across, down = (lax.broadcasted_iota(jnp.int32, (256, 256), n) for n in (1, 0))
        key_across = jnp.broadcast_to(key, (256, 256))
        key_down = key_across.T
        word_down = jnp.broadcast_to(slot | (where << 8), (256, 256)).T
        same = (key_across == key_down) & (across < down)
        less = (key_across < key_down) | same
        rank = jnp.sum(less.astype(jnp.int32), axis=1, keepdims=True)
        opens = jnp.sum(same.astype(jnp.int32), axis=1, keepdims=True) == 0
        word_down = word_down | (opens.astype(jnp.int32) << 16)
        upto = jnp.sum((key_down <= across).astype(jnp.int32), axis=0, keepdims=True)
        here = jnp.sum((key_down == across).astype(jnp.int32), axis=0, keepdims=True)
        table[...] = jnp.zeros((8, 256), jnp.int32)
        table[0:1, :] = jnp.sum(jnp.where(rank == across, word_down, 0), axis=0, keepdims=True)
        table[1:2, :] = jnp.where(here > 0, upto - 1, SLOTS)
        pltpu.sync_copy(table, lists)
        for load in loads[2:]:
            load.wait()

    steps = {
        "ring1": first_ring, "pass1": first_forward, "ring2": second_ring, "pass2": second_forward,
        "loads": wait_loads, "mult": multiply, "place": place, "z": z_step, "zend": z_end, "term": weight_term,
        "scatter": plane_scatter, "zsum": z_exchange, "gather": plane_gather, "core": core_gather,
        "out": weight_out, "rows": input_rows, "drain": drain,
    }
    for name, args in plan():
        steps[name](*args)
    drain(2)


def finish(ig, wg, ig_o, wg_o, sems):
    copies = [pltpu.make_async_copy(ig, ig_o, sems.at[0]), pltpu.make_async_copy(wg, wg_o, sems.at[1])]
    for copy in copies:
        copy.start()
    for copy in copies:
        copy.wait()


def local(out_grad, state, features, weight, block_values, block_rows, block_cols, block_counts):
    anywhere = pl.BlockSpec(memory_space=pl.ANY)
    dma = pltpu.SemaphoreType.DMA
    grid = (512, 512)
    ig, wg = pl.pallas_call(
        kernel,
        out_shape=(pltpu.VMEM(grid, BF), pltpu.VMEM(grid, F32)),
        in_specs=[pl.BlockSpec(memory_space=pltpu.SMEM)] + [pl.BlockSpec(memory_space=pltpu.VMEM)] * 2 + [anywhere] * 5,
        out_specs=(pl.BlockSpec(memory_space=pltpu.VMEM), pl.BlockSpec(memory_space=pltpu.VMEM)),
        scratch_shapes=[pltpu.VMEM((64, size, B), BF) for _, size in CUTS]
        + [pltpu.VMEM((8, 256), jnp.int32)] * 2
        + [pltpu.SMEM((8, 256), jnp.int32)]
        + [pltpu.VMEM(grid, BF)] * 4
        + [
            pltpu.VMEM((SLOTS, B, B), BF),
            pltpu.VMEM((SLOTS + 1, B, B), BF),
            pltpu.VMEM((B, B), F32),
            pltpu.VMEM((64, 512, B), BF),
            pltpu.VMEM((32, 512, B), BF),
            pltpu.VMEM((8, 4, 512, B), BF),
            pltpu.VMEM((8, 4, 512, B), BF),
            pltpu.VMEM((4, 512, B), BF),
            pltpu.VMEM((UNITS, B, 512), F32),
            pltpu.VMEM((UNITS, 64, 512), BF),
            pltpu.VMEM((UNITS, 64, 512), BF),
            pltpu.VMEM((UNITS, 16, 16, B), BF),
            pltpu.VMEM((UNITS, 15, 16, B), BF),
            pltpu.VMEM((UNITS, 8, 16, B), BF),
            pltpu.VMEM((UNITS, 2, 16, 16, B), BF),
            dma((5,)),
            dma((CHUNKS,)),
            dma((CHUNKS * 4,)),
            dma((CHUNKS,)),
            dma((CHUNKS * len(GROUPS),)),
            dma((CHUNKS,)),
            dma((CHUNKS * 7,)),
        ]
        + [dma((UNITS,))] * 10,
        compiler_params=pltpu.CompilerParams(
            collective_id=0, has_side_effects=True, vmem_limit_bytes=56 * 1024 * 1024
        ),
        name="graph_backward",
    )(block_counts, block_rows, block_cols, out_grad, state, features, weight, block_values[0, 0])
    return pl.pallas_call(
        finish,
        out_shape=(jax.ShapeDtypeStruct(grid, BF), jax.ShapeDtypeStruct(grid, F32)),
        in_specs=[pl.BlockSpec(memory_space=pltpu.VMEM)] * 2,
        out_specs=(anywhere, anywhere),
        scratch_shapes=[pltpu.SemaphoreType.DMA((2,))],
        name="finish",
    )(pltpu.with_memory_space_constraint(ig, pltpu.VMEM), pltpu.with_memory_space_constraint(wg, pltpu.VMEM))


def solution(mesh):
    in_specs = (
        P(("gr", "gc"), None),
        P(("gr", "gc"), None),
        P(("gc", "gr"), None),
        P(),
        P("gr", "gc", None, None, None),
        P("gr", "gc", None),
        P("gr", "gc", None),
        P("gr", "gc"),
    )
    out_specs = (P(("gc", "gr"), None), P())
    return jax.shard_map(local, mesh=mesh, in_specs=in_specs, out_specs=out_specs, check_vma=False)
```

```python
import functools

import jax
import jax.numpy as jnp
from jax import lax
from jax.experimental import pallas as pl
from jax.experimental.pallas import tpu as pltpu
from jax.sharding import PartitionSpec as P

MESH = pl.DeviceIdType.MESH
B = 128
SLOTS = 152
CUTS = ((0, 64), (64, 64), (128, 64), (192, 64), (256, 64), (320, 64), (384, 128))
CHUNKS = len(CUTS)
UNITS = 4
UNROLL = 76
BF = jnp.bfloat16
F32 = jnp.float32


GROUPS = ((4, 3, 5), (2, 6), (1, 7, 0))


def plan():
    tasks = {}

    def task(name, args, after=(), needs=(), sends=(), cost=0.1, rank=0.0):
        tasks[name, args] = (tuple(after), tuple(needs), tuple(sends), cost, rank)

    chip, core = 2.4, 0.9
    task("loads", (), cost=1.2, rank=-5)
    for k, (at, size) in enumerate(CUTS):
        unit = size / 2
        task("ring1", (k,), [("ring1", (k - 1,))] if k else [], (), [(("r1", k), "xy", unit, chip)], rank=-9)
        task("pass1", (k,), [], [("r1", k)], [(("f1", k), "xy", unit / 2, chip)], rank=-8)
        before = max(0, k - 1 - (size <= 64))
        gate = [("pass2", (before,))] if k > 1 else []
        task(
            "ring2", (k,), gate + ([("ring2", (k - 1,))] if k else []), [("f1", k)],
            [(("a", k), "xy", unit * 2, chip), (("b", k), "xy", unit * 2, chip)], rank=-7,
        )
        task("pass2", (k,), [], [("a", k)], [(("f2", k), "xy", unit * 2, chip)], rank=-8)
        load = 0.95
        follow = [("place", (k - 1, GROUPS[-1]))] if k else [("loads", ())]
        task("mult", (k, 0), follow, [("b", k), ("f2", k)], cost=load, rank=k)
        task("mult", (k, 1), [("mult", (k, 0))], cost=load, rank=k)
        for i, group in enumerate(GROUPS):
            task(
                "place", (k, group), [("place", (k, GROUPS[i - 1])) if i else ("mult", (k, 1))], (),
                [(("e", k, d), "core", size, core) for d in group], 0.08 * len(group), k - 0.5,
            )
        for chain in range(2):
            for t in range(4 - chain, 0, -1):
                needs = [("e", k, d) for d in sorted({t, 8 - t})]
                if t < 4 - chain:
                    needs.append(("z", k, chain, t + 1))
                task("z", (k, chain, t), (), needs, [(("z", k, chain, t), "z", size / 2, chip)], 0.2, -6 + k / 10)
        task("zend", (k,), (), [("e", k, 0), ("z", k, 0, 1), ("z", k, 1, 1)], cost=0.25, rank=-5 + k / 10)
    for u in range(UNITS):
        ends = [("zend", (k,)) for k, (at, _) in enumerate(CUTS) if at // B == u]
        task("term", (u,), ends, (), [(("t", u), "core", 64, core)], 0.7, u - 1)
        task("scatter", (u,), (), [("t", u)], [(("p", u), "xy", 32, 4.5)], 0.5, u - 1)
        behind = [("z", (CHUNKS - 1, 0, 1))] if u < UNITS - 1 else []
        task("zsum", (u,), behind, [("p", u)], [(("x", u), "z", 32, 4.5)], 0.4, u - 1)
        task("gather", (u,), (), [("x", u)], [(("q", u), "xy", 32, 4.5)], 0.5, u - 1)
        task("core", (u,), (), [("q", u)], [(("c", u), "core", 64, core)], 0.2, u - 1)
        task("out", (u,), (), [("c", u)], cost=0.4, rank=u + 1)
    for b in range(4):
        task("rows", (b,), [("zend", (CHUNKS - 1,)), ("scatter", (UNITS - 1,))], cost=0.6, rank=20)
    sums = [("z", (k, chain, 1)) for k in range(CHUNKS) for chain in range(2)]
    task("drain", (0,), [*sums, ("scatter", (UNITS - 1,))], cost=1.0, rank=30)
    task("drain", (1,), [("gather", (u,)) for u in range(UNITS)], cost=0.5, rank=30)

    now, free, come, done, order = 0.0, {"xy": 0.0, "z": 0.0, "core": 0.0}, {}, set(), []
    rate = {"xy": 48.0, "z": 48.0, "core": 600.0}
    while tasks:
        best = None
        for key, (after, needs, _, cost, rank) in tasks.items():
            if all(a in done for a in after) and all(n in come for n in needs):
                ready = max([now] + [come[n] for n in needs])
                score = (ready, rank)
                if best is None or score < best[0]:
                    best = (score, key)
        (now, _), key = best
        _, _, sends, cost, _ = tasks.pop(key)
        now += cost
        for message, link, kib, latency in sends:
            free[link] = max(free[link], now) + kib / rate[link]
            come[message] = free[link] + latency
        done.add(key)
        order.append(key)
    return order


def kernel(
    count, row_ids, col_ids, og_h, pre_h, feat_h, w_h, vals_h,
    ig_o, wg_o,
    g0, g1, g2, g3, g4, g5, g6, ids, table, lists, og, pre, feat, w, vals, prods, carry, part, sib, zs, zr, spread, term, tsend, trecv,
    psend, precv, zx, wg,
    local_sem, g_send, g_recv, e_send, e_recv, z_send, z_recv, t_send, t_recv, p_send, p_recv,
    x_send, x_recv, q_send, q_recv, c_send, c_recv,
):
    gathered = (g0, g1, g2, g3, g4, g5, g6)
    gr, gc = lax.axis_index("gr"), lax.axis_index("gc")
    scale = (512 * lax.axis_size("gr") * lax.axis_size("gc")) ** (-0.5)
    z, core = gr // 2, gr % 2
    x, y = gc // 4, gc % 4
    sibling = {"gr": z * 2 + (1 - core), "gc": gc}

    def z_peer(d):
        return {"gr": ((z + d) % 8) * 2 + core, "gc": gc}

    def plane_peer(d):
        return {"gr": gr, "gc": (gc + d) % 16}

    def x_peer(d):
        return {"gr": gr, "gc": ((x + d + 4) % 4) * 4 + y}

    def y_peer(d):
        return {"gr": gr, "gc": x * 4 + (y + d + 4) % 4}

    strips = []
    for k in range(UNITS):
        lanes = pl.ds(k * B, B)
        strips.append([
            pltpu.make_async_copy(og_h.at[:, lanes], og.at[:, lanes], local_sem.at[2 * k]),
            pltpu.make_async_copy(pre_h.at[:, lanes], pre.at[:, lanes], local_sem.at[2 * k + 1]),
        ])
    loads = [
        pltpu.make_async_copy(vals_h, vals, local_sem.at[8]),
        pltpu.make_async_copy(feat_h, feat, local_sem.at[9]),
        pltpu.make_async_copy(w_h, w, local_sem.at[10]),
    ]
    for load in [*strips[0], *strips[1], *strips[2], *strips[3], *loads]:
        load.start()

    barrier = pltpu.get_barrier_semaphore()
    pl.semaphore_signal(barrier, inc=1, device_id=sibling, device_id_type=MESH)

    for device in (z_peer(1), z_peer(7), x_peer(1), x_peer(-1), y_peer(1), y_peer(-1)):
        pl.semaphore_signal(barrier, inc=1, device_id=device, device_id_type=MESH)

    ring = (x, y)
    cross = (y, x)
    near = (x_peer, y_peer)
    far = (y_peer, x_peer)

    def unit(h, p, q):
        return h * 32 + p * 8 + q * 2

    def mask(k):
        for load in strips[k]:
            load.wait()
        for b in range(4):
            rows, cols = pl.ds(b * B, B), pl.ds(k * B, B)
            block = og[rows, cols]
            block = jnp.where(pre[rows, cols].astype(F32) > 0, block.astype(F32), 0.0).T.astype(BF)
            h = b // 2
            for n, (at, size) in enumerate(CUTS):
                if at // B == k:
                    gathered[n][unit(h, cross[h], ring[h]) + b % 2] = block[at % B : at % B + size]

    mask(0)
    prods[SLOTS] = jnp.zeros((B, B), BF)
    pl.semaphore_wait(barrier, 7)

    def send(src, dst, send_sem, recv_sem, device):
        pltpu.make_async_remote_copy(
            src_ref=src, dst_ref=dst, send_sem=send_sem, recv_sem=recv_sem, device_id=device, device_id_type=MESH
        ).start()

    def bytes_of(ref, sem):
        return pltpu.make_async_remote_copy(
            src_ref=ref, dst_ref=ref, send_sem=sem, recv_sem=sem, device_id=sibling, device_id_type=MESH
        )

    def arrived(ref, sem):
        bytes_of(ref, sem).wait_recv()

    def left(ref, sem):
        bytes_of(ref, sem).wait_send()

    def gather_copy(stage, k, h, d, at, size, device):
        where = gathered[k].at[pl.ds(at, size)]
        send(where, where, g_send.at[0], g_recv.at[k * 4 + min(stage, 3)], device)

    def gather_arrived(k, stage, blocks):
        arrived(gathered[k].at[pl.ds(0, blocks)], g_recv.at[k * 4 + stage])

    def first_ring(k):
        at = CUTS[k][0]
        if at and at % B == 0:
            mask(at // B)
        for h in range(2):
            for d in (1, -1):
                gather_copy(0, k, h, d, unit(h, cross[h], ring[h]), 2, near[h](d))

    def first_forward(k):
        gather_arrived(k, 0, 8)
        for h in range(2):
            for d in (1, -1):
                came = (ring[h] - d + 4) % 4
                gather_copy(1, k, h, d, unit(h, cross[h], came) + (0 if d == 1 else 1), 1, near[h](d))

    def second_ring(k):
        gather_arrived(k, 1, 4)
        for part_no in range(2):
            for h in range(2):
                for d in (1, -1):
                    which = part_no if d == 1 else 1 - part_no
                    gather_copy(2 + part_no, k, h, d, unit(h, cross[h], 0) + 4 * which, 4, far[h](d))

    def second_forward(k):
        gather_arrived(k, 2, 16)
        for h in range(2):
            for d in (1, -1):
                came = (cross[h] - d + 4) % 4
                gather_copy(4, k, h, d, unit(h, came, 0) + (0 if d == 1 else 4), 4, far[h](d))

    def multiply(k, half):
        at, size = CUTS[k]
        source = gathered[k]
        if half == 0:
            gather_arrived(k, 3, 32)

        def some(t, total):
            for u in range(UNROLL):
                s = (half + t) * UNROLL + u
                word = lists[0, s]
                term_now = jnp.dot(source[(word >> 8) & 255], vals[word & 255], preferred_element_type=F32)
                total = jnp.where((word >> 16) != 0, term_now, total + term_now)
                prods[s, pl.ds(0, size)] = total.astype(BF)
            return total

        begin = jnp.zeros((size, B), F32) if half == 0 else carry[pl.ds(0, size), :]
        total = lax.fori_loop(0, SLOTS // UNROLL // 2, some, begin)
        if half == 0:
            carry[pl.ds(0, size), :] = total

    def place(k, group):
        at, size = CUTS[k]
        for d in group:
            zp = (z + d) % 8

            def one(j, _):
                part[zp * 8 + j, pl.ds(at, size)] = prods[lists[1, zp * 8 + j], pl.ds(0, size)]
                return 0

            lax.fori_loop(0, 8, one, 0, unroll=True)
            n = k * len(GROUPS) + GROUPS.index(group)
            send(
                part.at[pl.ds(zp * 8 + (1 - core) * 4, 4), pl.ds(at, size)],
                sib.at[pl.ds(zp * 4, 4), pl.ds(at, size)],
                e_send.at[0], e_recv.at[n], sibling,
            )

    exchanged = set()

    def own(k, d, b):
        group = next(n for n, members in enumerate(GROUPS) if d in members)
        if (k, group) not in exchanged:
            exchanged.add((k, group))
            arrived(sib.at[pl.ds(0, 4 * len(GROUPS[group])), pl.ds(*CUTS[k])], e_recv.at[k * len(GROUPS) + group])
        zp = (z + d) % 8
        cut = pl.ds(*CUTS[k])
        return part[zp * 8 + core * 4 + b, cut].astype(F32) + sib[zp * 4 + b, cut].astype(F32)

    def z_sem(k, chain, t):
        return z_recv.at[k * 7 + (t + 2 if chain == 0 else t - 1)]

    def z_step(k, chain, t):
        cut = pl.ds(*CUTS[k])
        fresh = t == 4 - chain
        if not fresh:
            arrived(zr.at[0, :, cut], z_sem(k, chain, t + 1))
        for side in range(2):
            h = side if chain == 0 else 1 - side
            d = 8 - t if side == 0 else t
            n = side * 4 + t - 1
            for b in (2 * h, 2 * h + 1):
                value = own(k, d, b)
                if not fresh:
                    value = value + zr[n + 1, b, cut].astype(F32)
                zs[n, b, cut] = value.astype(BF)
            blocks = pl.ds(2 * h, 2)
            send(
                zs.at[n, blocks, cut], zr.at[n, blocks, cut],
                z_send.at[0], z_sem(k, chain, t), z_peer(7 if side == 0 else 1),
            )

    def z_end(k):
        cut = pl.ds(*CUTS[k])
        for chain in range(2):
            arrived(zr.at[0, :, cut], z_sem(k, chain, 1))
        for b in range(4):
            total = own(k, 0, b) + zr[0, b, cut].astype(F32) + zr[4, b, cut].astype(F32)
            spread[b, cut] = total.astype(BF)

    def weight_term(k):
        total = jnp.dot(spread[0, pl.ds(k * B, B)], feat[pl.ds(0, B), :], preferred_element_type=F32)
        for b in range(1, 4):
            rows = spread[b, pl.ds(k * B, B)]
            total = total + jnp.dot(rows, feat[pl.ds(b * B, B), :], preferred_element_type=F32)
        term[k] = total
        tsend[k] = term[k, pl.ds((1 - core) * 64, 64), :].astype(BF)
        send(tsend.at[k], trecv.at[k], t_send.at[0], t_recv.at[k], sibling)

    def plane_scatter(k):
        arrived(trecv.at[k], t_recv.at[k])
        for a in range(4):
            for b in range(4):
                lanes = pl.ds(b * B, B)
                mine = term[k, pl.ds(core * 64 + a * 16, 16), lanes]
                psend[k, a * 4 + b] = (mine + trecv[k, pl.ds(a * 16, 16), lanes].astype(F32)).astype(BF)
        for o in range(1, 16):
            to = plane_peer(o)
            send(psend.at[k, to["gc"]], precv.at[k, o - 1], p_send.at[0], p_recv.at[k], to)

    def z_exchange(k):
        arrived(precv.at[k], p_recv.at[k])
        total = psend[k, gc].astype(F32)
        for o in range(1, 16):
            total = total + precv[k, o - 1].astype(F32)
        zx[k, z] = total.astype(BF)
        for o in range(1, 8):
            send(zx.at[k, z], zx.at[k, z], x_send.at[0], x_recv.at[k], z_peer(o))

    def plane_gather(k):
        arrived(zx.at[k, pl.ds(0, 7)], x_recv.at[k])
        total = zx[k, 0].astype(F32)
        for a in range(1, 8):
            total = total + zx[k, a].astype(F32)
        wg[k, core, gc] = total.astype(BF)
        for o in range(1, 16):
            send(wg.at[k, core, gc], wg.at[k, core, gc], q_send.at[0], q_recv.at[k], plane_peer(o))

    def core_gather(k):
        arrived(wg.at[k, core, pl.ds(0, 15)], q_recv.at[k])
        send(wg.at[k, core], wg.at[k, core], c_send.at[0], c_recv.at[k], sibling)

    def weight_out(k):
        arrived(wg.at[k, core], c_recv.at[k])
        for b in range(4):
            rows = [wg[k, c, a * 4 + b] for c in range(2) for a in range(4)]
            whole = jnp.concatenate(rows, axis=0).astype(F32)
            wg_o[pl.ds(b * B, B), pl.ds(k * B, B)] = whole.T * scale

    def input_rows(b):
        total = lax.dot_general(spread[b].T, w[...], (((1,), (1,)), ((), ())), preferred_element_type=F32)
        ig_o[pl.ds(b * B, B), :] = total.astype(BF)

    def drain(stage):
        if stage == 0:
            left(part.at[pl.ds(0, 60)], g_send.at[0])
            left(sib, e_send.at[0])
            left(zs.at[pl.ds(0, 7)], z_send.at[0])
        elif stage == 1:
            left(tsend, t_send.at[0])
            left(precv, p_send.at[0])
            left(zx.at[:, pl.ds(0, 7)], x_send.at[0])
        else:
            left(precv, q_send.at[0])
            left(wg.at[:, core], c_send.at[0])

    def wait_loads():
        ids[...] = jnp.zeros((8, 256), jnp.int32)
        ids[0:1, 0:SLOTS] = row_ids[0]
        ids[1:2, 0:SLOTS] = col_ids[0]
        slot, row = lax.broadcasted_iota(jnp.int32, (1, 256), 1), ids[0:1, :]
        quarter, device = row & 3, row >> 2
        a0, a1 = device >> 2, device & 3
        where = jnp.where(quarter < 2, a1 * 8 + a0 * 2 + quarter, 32 + a0 * 8 + a1 * 2 + quarter - 2)
        key = jnp.where(slot < count[0, 0], ids[1:2, :], 64)
        across, down = (lax.broadcasted_iota(jnp.int32, (256, 256), n) for n in (1, 0))
        key_across = jnp.broadcast_to(key, (256, 256))
        key_down = key_across.T
        word_down = jnp.broadcast_to(slot | (where << 8), (256, 256)).T
        same = (key_across == key_down) & (across < down)
        less = (key_across < key_down) | same
        rank = jnp.sum(less.astype(jnp.int32), axis=1, keepdims=True)
        opens = jnp.sum(same.astype(jnp.int32), axis=1, keepdims=True) == 0
        word_down = word_down | (opens.astype(jnp.int32) << 16)
        upto = jnp.sum((key_down <= across).astype(jnp.int32), axis=0, keepdims=True)
        here = jnp.sum((key_down == across).astype(jnp.int32), axis=0, keepdims=True)
        table[...] = jnp.zeros((8, 256), jnp.int32)
        table[0:1, :] = jnp.sum(jnp.where(rank == across, word_down, 0), axis=0, keepdims=True)
        table[1:2, :] = jnp.where(here > 0, upto - 1, SLOTS)
        pltpu.sync_copy(table, lists)
        for load in loads:
            load.wait()

    steps = {
        "ring1": first_ring, "pass1": first_forward, "ring2": second_ring, "pass2": second_forward,
        "loads": wait_loads, "mult": multiply, "place": place, "z": z_step, "zend": z_end, "term": weight_term,
        "scatter": plane_scatter, "zsum": z_exchange, "gather": plane_gather, "core": core_gather,
        "out": weight_out, "rows": input_rows, "drain": drain,
    }
    for name, args in plan():
        steps[name](*args)
    drain(2)


def finish(ig, wg, ig_o, wg_o, sems):
    copies = [pltpu.make_async_copy(ig, ig_o, sems.at[0]), pltpu.make_async_copy(wg, wg_o, sems.at[1])]
    for copy in copies:
        copy.start()
    for copy in copies:
        copy.wait()


def local(out_grad, state, features, weight, block_values, block_rows, block_cols, block_counts):
    anywhere = pl.BlockSpec(memory_space=pl.ANY)
    dma = pltpu.SemaphoreType.DMA
    grid = (512, 512)
    ig, wg = pl.pallas_call(
        kernel,
        out_shape=(pltpu.VMEM(grid, BF), pltpu.VMEM(grid, F32)),
        in_specs=[pl.BlockSpec(memory_space=pltpu.SMEM)] + [pl.BlockSpec(memory_space=pltpu.VMEM)] * 2 + [anywhere] * 5,
        out_specs=(pl.BlockSpec(memory_space=pltpu.VMEM), pl.BlockSpec(memory_space=pltpu.VMEM)),
        scratch_shapes=[pltpu.VMEM((64, size, B), BF) for _, size in CUTS]
        + [pltpu.VMEM((8, 256), jnp.int32)] * 2
        + [pltpu.SMEM((8, 256), jnp.int32)]
        + [pltpu.VMEM(grid, BF)] * 4
        + [
            pltpu.VMEM((SLOTS, B, B), BF),
            pltpu.VMEM((SLOTS + 1, B, B), BF),
            pltpu.VMEM((B, B), F32),
            pltpu.VMEM((64, 512, B), BF),
            pltpu.VMEM((32, 512, B), BF),
            pltpu.VMEM((8, 4, 512, B), BF),
            pltpu.VMEM((8, 4, 512, B), BF),
            pltpu.VMEM((4, 512, B), BF),
            pltpu.VMEM((UNITS, B, 512), F32),
            pltpu.VMEM((UNITS, 64, 512), BF),
            pltpu.VMEM((UNITS, 64, 512), BF),
            pltpu.VMEM((UNITS, 16, 16, B), BF),
            pltpu.VMEM((UNITS, 15, 16, B), BF),
            pltpu.VMEM((UNITS, 8, 16, B), BF),
            pltpu.VMEM((UNITS, 2, 16, 16, B), BF),
            dma((11,)),
            dma((1,)),
            dma((CHUNKS * 4,)),
            dma((1,)),
            dma((CHUNKS * len(GROUPS),)),
            dma((1,)),
            dma((CHUNKS * 7,)),
        ]
        + [dma((1,)), dma((UNITS,))] * 5,
        compiler_params=pltpu.CompilerParams(
            collective_id=0, has_side_effects=True, vmem_limit_bytes=56 * 1024 * 1024
        ),
        name="graph_backward",
    )(block_counts, block_rows, block_cols, out_grad, state, features, weight, block_values[0, 0])
    return pl.pallas_call(
        finish,
        out_shape=(jax.ShapeDtypeStruct(grid, BF), jax.ShapeDtypeStruct(grid, F32)),
        in_specs=[pl.BlockSpec(memory_space=pltpu.VMEM)] * 2,
        out_specs=(anywhere, anywhere),
        scratch_shapes=[pltpu.SemaphoreType.DMA((2,))],
        name="finish",
    )(pltpu.with_memory_space_constraint(ig, pltpu.VMEM), pltpu.with_memory_space_constraint(wg, pltpu.VMEM))


def solution(mesh):
    in_specs = (
        P(("gr", "gc"), None),
        P(("gr", "gc"), None),
        P(("gc", "gr"), None),
        P(),
        P("gr", "gc", None, None, None),
        P("gr", "gc", None),
        P("gr", "gc", None),
        P("gr", "gc"),
    )
    out_specs = (P(("gc", "gr"), None), P())
    return jax.shard_map(local, mesh=mesh, in_specs=in_specs, out_specs=out_specs, check_vma=False)
```

```python
import functools

import jax
import jax.numpy as jnp
from jax import lax
from jax.experimental import pallas as pl
from jax.experimental.pallas import tpu as pltpu
from jax.sharding import PartitionSpec as P

MESH = pl.DeviceIdType.MESH
B = 128
SLOTS = 152
CUTS = ((0, 64), (64, 64), (128, 64), (192, 64), (256, 64), (320, 64), (384, 128))
CHUNKS = len(CUTS)
UNITS = 4
UNROLL = 76
BF = jnp.bfloat16
F32 = jnp.float32


GROUPS = ((4, 3, 5), (2, 6), (1, 7, 0))


def plan():
    tasks = {}

    def task(name, args, after=(), needs=(), sends=(), cost=0.1, rank=0.0):
        tasks[name, args] = (tuple(after), tuple(needs), tuple(sends), cost, rank)

    chip, core = 2.2, 0.9
    task("loads", (), cost=1.2, rank=-7.5)
    for k, (at, size) in enumerate(CUTS):
        unit = size / 2
        task("ring1", (k,), [("ring1", (k - 1,))] if k else [], (), [(("r1", k), "xy", unit, chip)], rank=-9)
        task("pass1", (k,), [], [("r1", k)], [(("f1", k), "xy", unit / 2, chip)], rank=-8)
        before = max(0, k - 1 - (size <= 64))
        gate = [("pass2", (before,))] if k > 1 else []
        task(
            "ring2", (k,), gate + ([("ring2", (k - 1,))] if k else []), [("f1", k)],
            [(("a", k), "xy", unit * 2, chip), (("b", k), "xy", unit * 2, chip)], rank=-7,
        )
        task("pass2", (k,), [], [("a", k)], [(("f2", k), "xy", unit * 2, chip)], rank=-8)
        load = 0.95
        follow = [("place", (k - 1, GROUPS[-1]))] if k else [("loads", ())]
        task("mult", (k, 0), follow, [("b", k), ("f2", k)], cost=load, rank=k)
        task("mult", (k, 1), [("mult", (k, 0))], cost=load, rank=k)
        for i, group in enumerate(GROUPS):
            task(
                "place", (k, group), [("place", (k, GROUPS[i - 1])) if i else ("mult", (k, 1))], (),
                [(("e", k, d), "core", size, core) for d in group], 0.08 * len(group), k - 0.5,
            )
        for chain in range(2):
            for t in range(4 - chain, 0, -1):
                needs = [("e", k, d) for d in sorted({t, 8 - t})]
                if t < 4 - chain:
                    needs.append(("z", k, chain, t + 1))
                task("z", (k, chain, t), (), needs, [(("z", k, chain, t), "z", size / 2, chip)], 0.2, -6 + k / 10)
        task("zend", (k,), (), [("e", k, 0), ("z", k, 0, 1), ("z", k, 1, 1)], cost=0.25, rank=-5 + k / 10)
    for u in range(UNITS):
        ends = [("zend", (k,)) for k, (at, _) in enumerate(CUTS) if at // B == u]
        task("term", (u,), ends, (), [(("t", u), "core", 64, core)], 0.7, u - 1)
        task("scatter", (u,), (), [("t", u)], [(("p", u), "xy", 32, 4.5)], 0.5, u - 1)
        behind = [("z", (CHUNKS - 1, 0, 1))] if u < UNITS - 1 else []
        task("zsum", (u,), behind, [("p", u)], [(("x", u), "z", 32, 4.5)], 0.4, u - 1)
        task("gather", (u,), (), [("x", u)], [(("q", u), "xy", 32, 4.5)], 0.5, u - 1)
        task("core", (u,), (), [("q", u)], [(("c", u), "core", 64, core)], 0.2, u - 1)
        task("out", (u,), (), [("c", u)], cost=0.4, rank=u + 1)
    for b in range(4):
        task("rows", (b,), [("zend", (CHUNKS - 1,)), ("scatter", (UNITS - 1,))], cost=0.6, rank=20)
    sums = [("z", (k, chain, 1)) for k in range(CHUNKS) for chain in range(2)]
    task("drain", (0,), [*sums, ("scatter", (UNITS - 1,))], cost=1.0, rank=30)
    task("drain", (1,), [("gather", (u,)) for u in range(UNITS)], cost=0.5, rank=30)

    now, free, come, done, order = 0.0, {"xy": 0.0, "z": 0.0, "core": 0.0}, {}, set(), []
    rate = {"xy": 48.0, "z": 48.0, "core": 600.0}
    while tasks:
        best = None
        for key, (after, needs, _, cost, rank) in tasks.items():
            if all(a in done for a in after) and all(n in come for n in needs):
                ready = max([now] + [come[n] for n in needs])
                score = (ready, rank)
                if best is None or score < best[0]:
                    best = (score, key)
        (now, _), key = best
        _, _, sends, cost, _ = tasks.pop(key)
        now += cost
        for message, link, kib, latency in sends:
            free[link] = max(free[link], now) + kib / rate[link]
            come[message] = free[link] + latency
        done.add(key)
        order.append(key)
    return order


def kernel(
    count, row_ids, col_ids, og_h, pre_h, feat_h, w_h, vals_h,
    ig_o, wg_o,
    g0, g1, g2, g3, g4, g5, g6, ids, table, lists, og, pre, feat, w, vals, prods, carry, part, sib, zs, zr, spread, term, tsend, trecv,
    psend, precv, zx, wg,
    local_sem, g_send, g_recv, e_send, e_recv, z_send, z_recv, t_send, t_recv, p_send, p_recv,
    x_send, x_recv, q_send, q_recv, c_send, c_recv,
):
    gathered = (g0, g1, g2, g3, g4, g5, g6)
    gr, gc = lax.axis_index("gr"), lax.axis_index("gc")
    scale = (512 * lax.axis_size("gr") * lax.axis_size("gc")) ** (-0.5)
    z, core = gr // 2, gr % 2
    x, y = gc // 4, gc % 4
    sibling = {"gr": z * 2 + (1 - core), "gc": gc}

    def z_peer(d):
        return {"gr": ((z + d) % 8) * 2 + core, "gc": gc}

    def plane_peer(d):
        return {"gr": gr, "gc": (gc + d) % 16}

    def x_peer(d):
        return {"gr": gr, "gc": ((x + d + 4) % 4) * 4 + y}

    def y_peer(d):
        return {"gr": gr, "gc": x * 4 + (y + d + 4) % 4}

    strips = []
    for k in range(UNITS):
        lanes = pl.ds(k * B, B)
        strips.append([
            pltpu.make_async_copy(og_h.at[:, lanes], og.at[:, lanes], local_sem.at[2 * k]),
            pltpu.make_async_copy(pre_h.at[:, lanes], pre.at[:, lanes], local_sem.at[2 * k + 1]),
        ])
    loads = [
        pltpu.make_async_copy(vals_h, vals, local_sem.at[8]),
        pltpu.make_async_copy(feat_h, feat, local_sem.at[9]),
        pltpu.make_async_copy(w_h, w, local_sem.at[10]),
    ]
    for load in [*strips[0], *strips[1], *strips[2], *strips[3], *loads]:
        load.start()

    barrier = pltpu.get_barrier_semaphore()
    pl.semaphore_signal(barrier, inc=1, device_id=sibling, device_id_type=MESH)

    for device in (z_peer(1), z_peer(7), x_peer(1), x_peer(-1), y_peer(1), y_peer(-1)):
        pl.semaphore_signal(barrier, inc=1, device_id=device, device_id_type=MESH)

    ring = (x, y)
    cross = (y, x)
    near = (x_peer, y_peer)
    far = (y_peer, x_peer)

    def unit(h, p, q):
        return h * 32 + p * 8 + q * 2

    def mask(k):
        for load in strips[k]:
            load.wait()
        for b in range(4):
            rows, cols = pl.ds(b * B, B), pl.ds(k * B, B)
            block = og[rows, cols]
            block = jnp.where(pre[rows, cols].astype(F32) > 0, block.astype(F32), 0.0).T.astype(BF)
            h = b // 2
            for n, (at, size) in enumerate(CUTS):
                if at // B == k:
                    gathered[n][unit(h, cross[h], ring[h]) + b % 2] = block[at % B : at % B + size]

    mask(0)
    prods[SLOTS] = jnp.zeros((B, B), BF)
    pl.semaphore_wait(barrier, 7)

    def send(src, dst, send_sem, recv_sem, device):
        pltpu.make_async_remote_copy(
            src_ref=src, dst_ref=dst, send_sem=send_sem, recv_sem=recv_sem, device_id=device, device_id_type=MESH
        ).start()

    def bytes_of(ref, sem):
        return pltpu.make_async_remote_copy(
            src_ref=ref, dst_ref=ref, send_sem=sem, recv_sem=sem, device_id=sibling, device_id_type=MESH
        )

    def arrived(ref, sem):
        bytes_of(ref, sem).wait_recv()

    def left(ref, sem):
        bytes_of(ref, sem).wait_send()

    def gather_copy(stage, k, h, d, at, size, device):
        where = gathered[k].at[pl.ds(at, size)]
        send(where, where, g_send.at[0], g_recv.at[k * 4 + min(stage, 3)], device)

    def gather_arrived(k, stage, blocks):
        arrived(gathered[k].at[pl.ds(0, blocks)], g_recv.at[k * 4 + stage])

    def first_ring(k):
        at = CUTS[k][0]
        if at and at % B == 0:
            mask(at // B)
        for h in range(2):
            for d in (1, -1):
                gather_copy(0, k, h, d, unit(h, cross[h], ring[h]), 2, near[h](d))

    def first_forward(k):
        gather_arrived(k, 0, 8)
        for h in range(2):
            for d in (1, -1):
                came = (ring[h] - d + 4) % 4
                gather_copy(1, k, h, d, unit(h, cross[h], came) + (0 if d == 1 else 1), 1, near[h](d))

    def second_ring(k):
        gather_arrived(k, 1, 4)
        for part_no in range(2):
            for h in range(2):
                for d in (1, -1):
                    which = part_no if d == 1 else 1 - part_no
                    gather_copy(2 + part_no, k, h, d, unit(h, cross[h], 0) + 4 * which, 4, far[h](d))

    def second_forward(k):
        gather_arrived(k, 2, 16)
        for h in range(2):
            for d in (1, -1):
                came = (cross[h] - d + 4) % 4
                gather_copy(4, k, h, d, unit(h, came, 0) + (0 if d == 1 else 4), 4, far[h](d))

    def multiply(k, half):
        at, size = CUTS[k]
        source = gathered[k]
        if half == 0:
            gather_arrived(k, 3, 32)

        def some(t, total):
            for u in range(UNROLL):
                s = (half + t) * UNROLL + u
                word = lists[0, s]
                term_now = jnp.dot(source[(word >> 8) & 255], vals[word & 255], preferred_element_type=F32)
                total = jnp.where((word >> 16) != 0, term_now, total + term_now)
                prods[s, pl.ds(0, size)] = total.astype(BF)
            return total

        begin = jnp.zeros((size, B), F32) if half == 0 else carry[pl.ds(0, size), :]
        total = lax.fori_loop(0, SLOTS // UNROLL // 2, some, begin)
        if half == 0:
            carry[pl.ds(0, size), :] = total

    def place(k, group):
        at, size = CUTS[k]
        for d in group:
            zp = (z + d) % 8

            def one(j, _):
                part[zp * 8 + j, pl.ds(at, size)] = prods[lists[1, zp * 8 + j], pl.ds(0, size)]
                return 0

            lax.fori_loop(0, 8, one, 0, unroll=True)
            n = k * len(GROUPS) + GROUPS.index(group)
            send(
                part.at[pl.ds(zp * 8 + (1 - core) * 4, 4), pl.ds(at, size)],
                sib.at[pl.ds(zp * 4, 4), pl.ds(at, size)],
                e_send.at[0], e_recv.at[n], sibling,
            )

    exchanged = set()

    def own(k, d, b):
        group = next(n for n, members in enumerate(GROUPS) if d in members)
        if (k, group) not in exchanged:
            exchanged.add((k, group))
            arrived(sib.at[pl.ds(0, 4 * len(GROUPS[group])), pl.ds(*CUTS[k])], e_recv.at[k * len(GROUPS) + group])
        zp = (z + d) % 8
        cut = pl.ds(*CUTS[k])
        return part[zp * 8 + core * 4 + b, cut].astype(F32) + sib[zp * 4 + b, cut].astype(F32)

    def z_sem(k, chain, t):
        return z_recv.at[k * 7 + (t + 2 if chain == 0 else t - 1)]

    def z_step(k, chain, t):
        cut = pl.ds(*CUTS[k])
        fresh = t == 4 - chain
        if not fresh:
            arrived(zr.at[0, :, cut], z_sem(k, chain, t + 1))
        for side in range(2):
            h = side if chain == 0 else 1 - side
            d = 8 - t if side == 0 else t
            n = side * 4 + t - 1
            for b in (2 * h, 2 * h + 1):
                value = own(k, d, b)
                if not fresh:
                    value = value + zr[n + 1, b, cut].astype(F32)
                zs[n, b, cut] = value.astype(BF)
            blocks = pl.ds(2 * h, 2)
            send(
                zs.at[n, blocks, cut], zr.at[n, blocks, cut],
                z_send.at[0], z_sem(k, chain, t), z_peer(7 if side == 0 else 1),
            )

    def z_end(k):
        cut = pl.ds(*CUTS[k])
        for chain in range(2):
            arrived(zr.at[0, :, cut], z_sem(k, chain, 1))
        for b in range(4):
            total = own(k, 0, b) + zr[0, b, cut].astype(F32) + zr[4, b, cut].astype(F32)
            spread[b, cut] = total.astype(BF)

    def weight_term(k):
        total = jnp.dot(spread[0, pl.ds(k * B, B)], feat[pl.ds(0, B), :], preferred_element_type=F32)
        for b in range(1, 4):
            rows = spread[b, pl.ds(k * B, B)]
            total = total + jnp.dot(rows, feat[pl.ds(b * B, B), :], preferred_element_type=F32)
        term[k] = total
        tsend[k] = term[k, pl.ds((1 - core) * 64, 64), :].astype(BF)
        send(tsend.at[k], trecv.at[k], t_send.at[0], t_recv.at[k], sibling)

    def plane_scatter(k):
        arrived(trecv.at[k], t_recv.at[k])
        for a in range(4):
            for b in range(4):
                lanes = pl.ds(b * B, B)
                mine = term[k, pl.ds(core * 64 + a * 16, 16), lanes]
                psend[k, a * 4 + b] = (mine + trecv[k, pl.ds(a * 16, 16), lanes].astype(F32)).astype(BF)
        for o in range(1, 16):
            to = plane_peer(o)
            send(psend.at[k, to["gc"]], precv.at[k, o - 1], p_send.at[0], p_recv.at[k], to)

    def z_exchange(k):
        arrived(precv.at[k], p_recv.at[k])
        total = psend[k, gc].astype(F32)
        for o in range(1, 16):
            total = total + precv[k, o - 1].astype(F32)
        zx[k, z] = total.astype(BF)
        for o in range(1, 8):
            send(zx.at[k, z], zx.at[k, z], x_send.at[0], x_recv.at[k], z_peer(o))

    def plane_gather(k):
        arrived(zx.at[k, pl.ds(0, 7)], x_recv.at[k])
        total = zx[k, 0].astype(F32)
        for a in range(1, 8):
            total = total + zx[k, a].astype(F32)
        wg[k, core, gc] = total.astype(BF)
        for o in range(1, 16):
            send(wg.at[k, core, gc], wg.at[k, core, gc], q_send.at[0], q_recv.at[k], plane_peer(o))

    def core_gather(k):
        arrived(wg.at[k, core, pl.ds(0, 15)], q_recv.at[k])
        send(wg.at[k, core], wg.at[k, core], c_send.at[0], c_recv.at[k], sibling)

    def weight_out(k):
        arrived(wg.at[k, core], c_recv.at[k])
        for b in range(4):
            rows = [wg[k, c, a * 4 + b] for c in range(2) for a in range(4)]
            whole = jnp.concatenate(rows, axis=0).astype(F32)
            wg_o[pl.ds(b * B, B), pl.ds(k * B, B)] = whole.T * scale

    def input_rows(b):
        total = lax.dot_general(spread[b].T, w[...], (((1,), (1,)), ((), ())), preferred_element_type=F32)
        ig_o[pl.ds(b * B, B), :] = total.astype(BF)

    def drain(stage):
        if stage == 0:
            left(part.at[pl.ds(0, 60)], g_send.at[0])
            left(sib, e_send.at[0])
            left(zs.at[pl.ds(0, 7)], z_send.at[0])
        elif stage == 1:
            left(tsend, t_send.at[0])
            left(precv, p_send.at[0])
            left(zx.at[:, pl.ds(0, 7)], x_send.at[0])
        else:
            left(precv, q_send.at[0])
            left(wg.at[:, core], c_send.at[0])

    def wait_loads():
        ids[...] = jnp.zeros((8, 256), jnp.int32)
        ids[0:1, 0:SLOTS] = row_ids[0]
        ids[1:2, 0:SLOTS] = col_ids[0]
        slot, row = lax.broadcasted_iota(jnp.int32, (1, 256), 1), ids[0:1, :]
        quarter, device = row & 3, row >> 2
        a0, a1 = device >> 2, device & 3
        where = jnp.where(quarter < 2, a1 * 8 + a0 * 2 + quarter, 32 + a0 * 8 + a1 * 2 + quarter - 2)
        key = jnp.where(slot < count[0, 0], ids[1:2, :], 64)
        across, down = (lax.broadcasted_iota(jnp.int32, (256, 256), n) for n in (1, 0))
        key_across = jnp.broadcast_to(key, (256, 256))
        key_down = key_across.T
        word_down = jnp.broadcast_to(slot | (where << 8), (256, 256)).T
        same = (key_across == key_down) & (across < down)
        less = (key_across < key_down) | same
        rank = jnp.sum(less.astype(jnp.int32), axis=1, keepdims=True)
        opens = jnp.sum(same.astype(jnp.int32), axis=1, keepdims=True) == 0
        word_down = word_down | (opens.astype(jnp.int32) << 16)
        upto = jnp.sum((key_down <= across).astype(jnp.int32), axis=0, keepdims=True)
        here = jnp.sum((key_down == across).astype(jnp.int32), axis=0, keepdims=True)
        table[...] = jnp.zeros((8, 256), jnp.int32)
        table[0:1, :] = jnp.sum(jnp.where(rank == across, word_down, 0), axis=0, keepdims=True)
        table[1:2, :] = jnp.where(here > 0, upto - 1, SLOTS)
        pltpu.sync_copy(table, lists)
        for load in loads:
            load.wait()

    steps = {
        "ring1": first_ring, "pass1": first_forward, "ring2": second_ring, "pass2": second_forward,
        "loads": wait_loads, "mult": multiply, "place": place, "z": z_step, "zend": z_end, "term": weight_term,
        "scatter": plane_scatter, "zsum": z_exchange, "gather": plane_gather, "core": core_gather,
        "out": weight_out, "rows": input_rows, "drain": drain,
    }
    for name, args in plan():
        steps[name](*args)
    drain(2)


def finish(ig, wg, ig_o, wg_o, sems):
    copies = [pltpu.make_async_copy(ig, ig_o, sems.at[0]), pltpu.make_async_copy(wg, wg_o, sems.at[1])]
    for copy in copies:
        copy.start()
    for copy in copies:
        copy.wait()


def local(out_grad, state, features, weight, block_values, block_rows, block_cols, block_counts):
    anywhere = pl.BlockSpec(memory_space=pl.ANY)
    dma = pltpu.SemaphoreType.DMA
    grid = (512, 512)
    ig, wg = pl.pallas_call(
        kernel,
        out_shape=(pltpu.VMEM(grid, BF), pltpu.VMEM(grid, F32)),
        in_specs=[pl.BlockSpec(memory_space=pltpu.SMEM)] + [pl.BlockSpec(memory_space=pltpu.VMEM)] * 2 + [anywhere] * 5,
        out_specs=(pl.BlockSpec(memory_space=pltpu.VMEM), pl.BlockSpec(memory_space=pltpu.VMEM)),
        scratch_shapes=[pltpu.VMEM((64, size, B), BF) for _, size in CUTS]
        + [pltpu.VMEM((8, 256), jnp.int32)] * 2
        + [pltpu.SMEM((8, 256), jnp.int32)]
        + [pltpu.VMEM(grid, BF)] * 4
        + [
            pltpu.VMEM((SLOTS, B, B), BF),
            pltpu.VMEM((SLOTS + 1, B, B), BF),
            pltpu.VMEM((B, B), F32),
            pltpu.VMEM((64, 512, B), BF),
            pltpu.VMEM((32, 512, B), BF),
            pltpu.VMEM((8, 4, 512, B), BF),
            pltpu.VMEM((8, 4, 512, B), BF),
            pltpu.VMEM((4, 512, B), BF),
            pltpu.VMEM((UNITS, B, 512), F32),
            pltpu.VMEM((UNITS, 64, 512), BF),
            pltpu.VMEM((UNITS, 64, 512), BF),
            pltpu.VMEM((UNITS, 16, 16, B), BF),
            pltpu.VMEM((UNITS, 15, 16, B), BF),
            pltpu.VMEM((UNITS, 8, 16, B), BF),
            pltpu.VMEM((UNITS, 2, 16, 16, B), BF),
            dma((11,)),
            dma((1,)),
            dma((CHUNKS * 4,)),
            dma((1,)),
            dma((CHUNKS * len(GROUPS),)),
            dma((1,)),
            dma((CHUNKS * 7,)),
        ]
        + [dma((1,)), dma((UNITS,))] * 5,
        compiler_params=pltpu.CompilerParams(
            collective_id=0, has_side_effects=True, vmem_limit_bytes=56 * 1024 * 1024
        ),
        name="graph_backward",
    )(block_counts, block_rows, block_cols, out_grad, state, features, weight, block_values[0, 0])
    return pl.pallas_call(
        finish,
        out_shape=(jax.ShapeDtypeStruct(grid, BF), jax.ShapeDtypeStruct(grid, F32)),
        in_specs=[pl.BlockSpec(memory_space=pltpu.VMEM)] * 2,
        out_specs=(anywhere, anywhere),
        scratch_shapes=[pltpu.SemaphoreType.DMA((2,))],
        name="finish",
    )(pltpu.with_memory_space_constraint(ig, pltpu.VMEM), pltpu.with_memory_space_constraint(wg, pltpu.VMEM))


def solution(mesh):
    in_specs = (
        P(("gr", "gc"), None),
        P(("gr", "gc"), None),
        P(("gc", "gr"), None),
        P(),
        P("gr", "gc", None, None, None),
        P("gr", "gc", None),
        P("gr", "gc", None),
        P("gr", "gc"),
    )
    out_specs = (P(("gc", "gr"), None), P())
    return jax.shard_map(local, mesh=mesh, in_specs=in_specs, out_specs=out_specs, check_vma=False)
```
